256 devices in a mesh: sec: 64 (over z, x, core), pair: 4 (over y).
Axes of the slice: x: 4, y: 4, z: 8, core: 2. Of those that a mesh axis runs over, the one named last changes fastest.
Arguments:
- psi_start: float32 [64, 16, 128, 128], P('sec', 'pair'), may hold values from -6 to 6
- left_env: float32 [6, 64, 128, 128], P(None, 'sec')
- right_env: float32 [6, 16, 128, 128], P(None, 'pair')
- mpo_coef: float32 [6, 16, 16], replicated, may hold values from -0.625 to 0.625
- mpo_pattern: int32 [6, 16, 16], replicated, may hold values 0 or 1
- sector_shift: int32 [6], replicated, may hold values from -1 to 1, as said below
- block_rows: int32 [64], P('sec'), may hold values from 64 to 128, as said below
Outputs:
- state: float32 [64, 16, 128, 128], P('sec', 'pair')
- energies: float32 [4], replicated
The draws below stay inside these ranges and needn't reach their ends.
Inputs may be any that keep to these rules, and one draw needn't show every extreme that they name: `sector_shift`: each of -1, 0 and 1 occurs at least once. `block_rows`: some sector has all 128 rows.
All inputs are finite; a program needn't handle non-finite values.
Results may differ from the reference program's by a relative error of at most 0.0013.
Values sent between devices are 32-bit elements; how exact they have to be, the bound alone decides.
No kernel may reach another device: no remote copies, remote signals or barrier semaphores. Data moves between devices by JAX's collectives and lax.ppermute only.
A program may use at most 192 MiB of HBM per device.

```python
import jax
import jax.numpy as jnp
from jax import lax

B = 128
P_SIZE = 16
K = 6
ITERS = 4
SECTORS = 64


def dominant_blocks(key, shape):
    noise_key, diag_key = jax.random.split(key, 2)
    noise = jax.random.normal(noise_key, shape, jnp.float32)
    noise = noise / jnp.sqrt(jnp.float32(B))
    diag = jax.random.uniform(diag_key, shape[:-1], jnp.float32, 0.5, 2.5)
    eye = jnp.eye(B, dtype=jnp.float32)
    return noise + diag[..., None] * eye


def draw_left_env(key, part):
    key = jax.random.fold_in(key, 1)
    return dominant_blocks(key, (K, SECTORS, B, B))


def draw_right_env(key, part):
    key = jax.random.fold_in(key, 2)
    return dominant_blocks(key, (K, P_SIZE, B, B))


def draw_block_rows(key, part):
    key = jax.random.fold_in(key, 3)
    rows_key, place_key = jax.random.split(key)
    rows = jax.random.randint(rows_key, (SECTORS,), B // 2, B + 1)
    place = jax.random.randint(place_key, (), 0, SECTORS)
    return rows.at[place].set(B).astype(jnp.int32)


def draw_sector_shift(key, part):
    key = jax.random.fold_in(key, 4)
    extra_key, order_key = jax.random.split(key)
    base = jnp.array([-1, 0, 1], jnp.int32)
    extra = jax.random.randint(extra_key, (K - 3,), -1, 2).astype(jnp.int32)
    steps = jnp.concatenate([base, extra])
    order = jax.random.permutation(order_key, K)
    return steps[order].astype(jnp.int32)


def place_ends(result, key, low, largest):
    spot = [jax.random.randint(jax.random.fold_in(key, axis), (), 0, length) for axis, length in enumerate(result.shape)]
    widest = result.shape.index(max(result.shape))
    neighbour = spot[:widest] + [(spot[widest] + 1) % result.shape[widest]] + spot[widest + 1:]
    return result.at[tuple(spot)].set(low).at[tuple(neighbour)].set(largest)


def steps_of(key, extent, cuts, low, largest):
    factor_of, own = 1.0, jax.random.fold_in(key, 6)
    for dim, parts in cuts:
        heights = jnp.exp(jax.random.uniform(jax.random.fold_in(own, dim), (parts,), jnp.float32, low / len(cuts), largest / len(cuts)))
        factor_of = factor_of * jnp.repeat(heights, extent[dim] // parts).reshape([-1 if axis == dim else 1 for axis in range(len(extent))])
    return factor_of


def gaussian(own_key, extent, scale, limit, shards=(), kind=jnp.bfloat16):
    values = jax.random.normal(own_key, extent, jnp.float32) * scale
    if len(shards) > 0:
        values = steps_of(own_key, extent, shards, -0.22, 0.18) * values
    return jnp.clip(values, min=-limit, max=limit).astype(kind)


def setup_inputs(seed: int = 0) -> dict:
    arg_keys = jax.random.split(jax.random.key(seed), 8)
    return {
        "psi_start": gaussian(arg_keys[0], (SECTORS, P_SIZE, B, B), 1.0, 6.0, ((0, 64), (1, 4)), jnp.float32),
        "left_env": draw_left_env(jax.random.fold_in(arg_keys[7], 71), 0),
        "right_env": draw_right_env(jax.random.fold_in(arg_keys[7], 71), 0),
        "mpo_coef": gaussian(arg_keys[3], (K, P_SIZE, P_SIZE), (P_SIZE * K) ** -0.5, 0.625, (), jnp.float32),
        "mpo_pattern": place_ends((jax.random.randint(arg_keys[4], (K, P_SIZE, P_SIZE), 0, 4) < 3).astype(jnp.int32), jax.random.fold_in(arg_keys[4], 1), 0, 1),
        "sector_shift": draw_sector_shift(jax.random.fold_in(arg_keys[7], 71), 0),
        "block_rows": draw_block_rows(jax.random.fold_in(arg_keys[7], 71), 0),
    }


precise = lax.Precision.HIGHEST

def row_mask(block_rows):
    return (jnp.arange(B)[None, :] < block_rows[:, None]).astype(jnp.float32)

def apply_ham(vector, left_env, right_env, weights, sector_shift, mask):
    total = jnp.zeros(vector.shape, jnp.float32)
    for term in range(K):
        right_part = jnp.einsum('sqij,qlj->sqil', vector, right_env[term], precision=precise)
        mixed = jnp.einsum('pq,sqil->spil', weights[term], right_part, precision=precise)
        padded = jnp.pad(mixed, ((1, 1), (0, 0), (0, 0), (0, 0)))
        source = lax.dynamic_slice_in_dim(padded, (sector_shift[term] + 1).astype(jnp.int32), SECTORS, 0)
        total = total + jnp.einsum('sil,splj->spij', left_env[term], source, precision=precise)
    return total * mask[:, None, :, None]

def ham_diagonal(left_env, right_env, weights, sector_shift, mask):
    chosen = (sector_shift == 0).astype(jnp.float32)
    weight_diag = jnp.diagonal(weights, axis1=1, axis2=2) * chosen[:, None]
    left_diag = jnp.diagonal(left_env, axis1=2, axis2=3)
    right_diag = jnp.diagonal(right_env, axis1=2, axis2=3)
    diag = jnp.einsum('kp,ksi,kpj->spij', weight_diag, left_diag, right_diag, precision=precise)
    return diag * mask[:, None, :, None]

def lowest_root(lead, middle, const):
    root = jnp.sqrt(middle * middle - 4.0 * lead * const)
    return jnp.where(middle > 0, (-middle - root) / (2.0 * lead), 2.0 * const / (root - middle))

def reference(psi_start, left_env, right_env, mpo_coef, mpo_pattern, sector_shift, block_rows):
    mask = row_mask(block_rows)
    weights = mpo_coef * mpo_pattern.astype(jnp.float32)
    count = float(SECTORS * P_SIZE * B * B)
    diag = ham_diagonal(left_env, right_env, weights, sector_shift, mask)
    state = psi_start * mask[:, None, :, None]
    image = apply_ham(state, left_env, right_env, weights, sector_shift, mask)
    energies = []
    for step in range(ITERS):
        rayleigh = jnp.sum(state * image) / count
        length = jnp.sum(state * state) / count
        theta = rayleigh / length
        correction = (image - theta * state) / jnp.maximum(jnp.abs(diag - theta), 1.0)
        image_corr = apply_ham(correction, left_env, right_env, weights, sector_shift, mask)
        cross = 0.5 * (jnp.sum(state * image_corr) + jnp.sum(correction * image)) / count
        curvature = jnp.sum(correction * image_corr) / count
        correlation = jnp.sum(state * correction) / count
        spread = jnp.sum(correction * correction) / count
        lead = length * spread - correlation * correlation
        middle = -(length * curvature + spread * rayleigh - 2.0 * correlation * cross)
        const = rayleigh * curvature - cross * cross
        lowest = lowest_root(lead, middle, const)
        keep = curvature - lowest * spread
        add = lowest * correlation - cross
        factor = 1.0 / jnp.sqrt(keep * keep * length + 2.0 * keep * add * correlation + add * add * spread)
        state = (keep * state + add * correction) * factor
        image = (keep * image + add * image_corr) * factor
        energies.append(lowest)
    return (state, jnp.stack(energies))
```

```python
import jax
import jax.numpy as jnp
from jax import lax
from jax.experimental import pallas as pl
from jax.experimental.pallas import tpu as pltpu
from jax.sharding import PartitionSpec as P

ITERS = 4
TERMS = 6
LOCAL = 4
GROUPS = 4
B = 128
PACK = LOCAL * B + 8

f32 = jnp.float32
bf16 = jnp.bfloat16
VM = pl.BlockSpec(memory_space=pltpu.VMEM)
SM = pl.BlockSpec(memory_space=pltpu.SMEM)
PARAMS = pltpu.CompilerParams(vmem_limit_bytes=48 * 1024 * 1024)


def halves(x):
    high = x.astype(bf16)
    return high, (x - high.astype(f32)).astype(bf16)


def eye_mask():
    return lax.broadcasted_iota(jnp.int32, (B, B), 0) == lax.broadcasted_iota(jnp.int32, (B, B), 1)


def pack_kernel(shift, rows, psi, left, pack):
    keep = (lax.broadcasted_iota(jnp.int32, (B, B), 0) < rows[0]).astype(f32)
    for p in range(LOCAL):
        pack[p * B:(p + 1) * B, :] = psi[p] * keep
    eye = eye_mask()
    lines = []
    for k in range(TERMS):
        chosen = jnp.where(shift[k] == 0, 1.0, 0.0).astype(f32)
        diag = jnp.sum(jnp.where(eye, left[k] * keep, 0.0), axis=0, keepdims=True)
        lines.append(diag * chosen)
    lines.append(jnp.zeros((8 - TERMS, B), f32))
    pack[LOCAL * B:PACK, :] = jnp.concatenate(lines, axis=0)


def split_kernel(group, rows, weights, left, right, left2, right2, right_diag):
    keep = (lax.broadcasted_iota(jnp.int32, (B, B), 0) < rows[0]).astype(f32)
    eye = eye_mask()
    for k in range(TERMS):
        left2[k] = jnp.concatenate(halves(left[k] * keep), axis=1)
    for q in range(LOCAL):
        lines = []
        for k in range(TERMS):
            block = right[k, q]
            right2[k, q] = jnp.concatenate(halves(jnp.transpose(block)), axis=1)
            p = group[0] * LOCAL + q
            scale = weights[k * 256 + p * 16 + p]
            lines.append(jnp.sum(jnp.where(eye, block, 0.0), axis=0, keepdims=True) * scale)
        lines.append(jnp.zeros((8 - TERMS, B), f32))
        right_diag[q] = jnp.concatenate(lines, axis=0)


def partial_images(group, shift, weights, left2, right2, vec2, z, outs):
    def term(k, carry):
        source = shift[k] + 1
        lhs = left2[k]
        for q in range(LOCAL):
            r = right2[k, q]
            x = jnp.dot(vec2[source, q], jnp.concatenate([r, r], axis=0), preferred_element_type=f32)
            xh, xl = halves(x[:, :B] + x[:, B:])
            both = jnp.concatenate([xh, xl], axis=1)
            y = jnp.dot(lhs, jnp.concatenate([both, both], axis=0), preferred_element_type=f32)
            z[k * LOCAL + q] = y[:, :B] + y[:, B:]
        return carry

    lax.fori_loop(0, TERMS, term, 0)
    for step, out in enumerate(outs):
        base = lax.rem(group[0] + step, GROUPS) * LOCAL

        def pair(t, carry, out=out, base=base):
            first = base + 2 * t
            acc = [jnp.zeros((B, B), f32), jnp.zeros((B, B), f32)]
            for k in range(TERMS):
                for q in range(LOCAL):
                    block = z[k * LOCAL + q]
                    for j in range(2):
                        at = k * 256 + (first + j) * 16 + group[0] * LOCAL + q
                        acc[j] = acc[j] + weights[at] * block
            for j in range(2):
                out[2 * t + j] = acc[j]
            return carry

        lax.fori_loop(0, LOCAL // 2, pair, 0)


def first_kernel(group, shift, weights, pack, pack_low, pack_high, left2, right2, right_diag,
                 state3, diag3, out0, out1, out2, out3, vec2, z):
    for sector, src in enumerate((pack_low, pack, pack_high)):
        lines = src[LOCAL * B:PACK, :]
        for p in range(LOCAL):
            block = src[p * B:(p + 1) * B, :]
            state3[sector, p] = block
            vec2[sector, p] = jnp.concatenate(halves(block), axis=1)
            diag3[sector, p] = lax.dot_general(
                lines, right_diag[p], (((0,), (0,)), ((), ())),
                precision=lax.Precision.HIGHEST, preferred_element_type=f32)
    partial_images(group, shift, weights, left2, right2, vec2, z, (out0, out1, out2, out3))


def lane(row, j):
    at = lax.broadcasted_iota(jnp.int32, row.shape, 1) == j
    return jnp.sum(jnp.where(at, row, 0.0), axis=1, keepdims=True)


def put_lanes(values):
    at = lax.broadcasted_iota(jnp.int32, (1, B), 1)
    row = jnp.zeros((1, B), f32)
    for j, v in enumerate(values):
        row = jnp.where(at == j, v, row)
    return row


def lowest_root(lead, middle, const):
    root = jnp.sqrt(middle * middle - 4.0 * lead * const)
    return jnp.where(middle > 0, (-middle - root) / (2.0 * lead), 2.0 * const / (root - middle))


def ritz(sums, rayleigh, length):
    s_ic, c_i, curvature, correlation, spread = sums
    cross = 0.5 * (s_ic + c_i)
    lead = length * spread - correlation * correlation
    middle = -(length * curvature + spread * rayleigh - 2.0 * correlation * cross)
    const = rayleigh * curvature - cross * cross
    lowest = lowest_root(lead, middle, const)
    keep = curvature - lowest * spread
    add = lowest * correlation - cross
    norm = keep * keep * length + 2.0 * keep * add * correlation + add * add * spread
    factor = 1.0 / jnp.sqrt(norm)
    keep, add = keep * factor, add * factor
    rayleigh = keep * keep * rayleigh + 2.0 * keep * add * cross + add * add * curvature
    length = keep * keep * length + 2.0 * keep * add * correlation + add * add * spread
    return lowest, keep, add, rayleigh, length


def totals(stats, count, n):
    row = jnp.sum(stats[...], axis=0, keepdims=True) * (1.0 / count)
    return [lane(row, j) for j in range(n)]


def correct(state, image, diag, theta):
    return (image - theta * state) / jnp.maximum(jnp.abs(diag - theta), 1.0)


def start_kernel(count, group, shift, weights, stats, state3, diag3, image, image_low, image_high, left2, right2,
                 corr3, carry, out0, out1, out2, out3, vec2, z):
    rayleigh, length = totals(stats, count, 2)
    theta = rayleigh / length
    for sector, src in enumerate((image_low, image, image_high)):
        for p in range(LOCAL):
            c = correct(state3[sector, p], src[p], diag3[sector, p], theta)
            corr3[sector, p] = c
            vec2[sector, p] = jnp.concatenate(halves(c), axis=1)
    carry[...] = jnp.broadcast_to(put_lanes([rayleigh, length]), (8, B))
    partial_images(group, shift, weights, left2, right2, vec2, z, (out0, out1, out2, out3))


def next_kernel(count, step, group, shift, weights, stats, carry_in, state3, diag3, corr3,
                im_low, im_own, im_high, add_low, add_own, add_high, left2, right2,
                state_out, image_out, corr_out, carry, out0, out1, out2, out3, vec2, z):
    sums = totals(stats, count, 5)
    old = carry_in[0:1, :]
    lowest, keep, add, rayleigh, length = ritz(sums, lane(old, 0), lane(old, 1))
    theta = rayleigh / length
    images = ((im_low, add_low), (im_own, add_own), (im_high, add_high))
    for sector, (im, more) in enumerate(images):
        for p in range(LOCAL):
            s = keep * state3[sector, p] + add * corr3[sector, p]
            i = keep * im[p] + add * more[p]
            c = correct(s, i, diag3[sector, p], theta)
            state_out[sector, p] = s
            image_out[sector, p] = i
            corr_out[sector, p] = c
            vec2[sector, p] = jnp.concatenate(halves(c), axis=1)
    energies = [lane(old, 2 + j) for j in range(step)] + [lowest]
    carry[...] = jnp.broadcast_to(put_lanes([rayleigh, length] + energies), (8, B))
    partial_images(group, shift, weights, left2, right2, vec2, z, (out0, out1, out2, out3))


def last_kernel(count, stats, carry_in, state, corr, state_out, energies):
    sums = totals(stats, count, 5)
    old = carry_in[0:1, :]
    lowest, keep, add, _, _ = ritz(sums, lane(old, 0), lane(old, 1))
    for p in range(LOCAL):
        state_out[p] = keep * state[0, p] + add * corr[0, p]
    row = put_lanes([lane(old, 2 + j) for j in range(ITERS - 1)] + [lowest])
    energies[...] = row


def sum_all(block):
    return jnp.sum(jnp.sum(block, axis=0, keepdims=True), axis=1, keepdims=True)


def first_stats_kernel(own, r1, r2, r3, state, image, stats):
    a, b = jnp.zeros((B, B), f32), jnp.zeros((B, B), f32)
    for p in range(LOCAL):
        i = (own[p] + r2[p]) + (r1[p] + r3[p])
        s = state[0, p]
        image[p] = i
        a = a + s * i
        b = b + s * s
    stats[...] = jnp.broadcast_to(put_lanes([sum_all(a), sum_all(b)]), stats.shape)


def stats_kernel(own, r1, r2, r3, state, corr, image, image_corr, stats):
    acc = [jnp.zeros((B, B), f32) for _ in range(5)]
    for p in range(LOCAL):
        ic = (own[p] + r2[p]) + (r1[p] + r3[p])
        s, c, i = state[0, p], corr[0, p], image[0, p]
        image_corr[p] = ic
        for j, v in enumerate((s * ic, c * i, c * ic, s * c, c * c)):
            acc[j] = acc[j] + v
    stats[...] = jnp.broadcast_to(put_lanes([sum_all(a) for a in acc]), stats.shape)


def arr(*shape, dtype=f32):
    return jax.ShapeDtypeStruct(shape, dtype)


BLOCK = arr(LOCAL, B, B)
BLOCK3 = arr(3, LOCAL, B, B)
SCRATCH = [pltpu.VMEM((3, LOCAL, B, 2 * B), bf16), pltpu.VMEM((TERMS * LOCAL, B, B), f32)]


def call(kernel, name, in_specs, outs, scratch=()):
    return pl.pallas_call(
        kernel,
        grid=(1,),
        out_shape=outs,
        in_specs=in_specs,
        out_specs=[VM] * len(outs),
        scratch_shapes=list(scratch),
        compiler_params=PARAMS,
        name=name,
    )


def ring(n, step):
    return [(i, (i + step) % n) for i in range(n)]


def reduce_pair(parts):
    return [lax.ppermute(parts[d], "pair", ring(GROUPS, d)) for d in (1, 2, 3)]


def from_neighbours(x):
    n = lax.axis_size("sec")
    low = lax.ppermute(x, "sec", [(i, i + 1) for i in range(n - 1)])
    high = lax.ppermute(x, "sec", [(i + 1, i) for i in range(n - 1)])
    return low, high


def exchange(stats, devices):
    got = lax.all_to_all(stats.reshape(devices, 1, B), ("sec", "pair"), 0, 0)
    return got.reshape(devices, B)


def middle(arity):
    return [pl.BlockSpec((1, LOCAL, B, B), lambda i: (1, 0, 0, 0))] * arity


def on_device(psi_start, left_env, right_env, mpo_coef, mpo_pattern, sector_shift, block_rows):
    devices = lax.axis_size("sec") * lax.axis_size("pair")
    count = float(psi_start.size * devices)
    psi = psi_start.reshape(LOCAL, B, B)
    left = left_env.reshape(TERMS, B, B)
    group = lax.axis_index("pair").astype(jnp.int32).reshape(1)
    weights = (mpo_coef * mpo_pattern.astype(f32)).reshape(-1)
    stats_shape = arr(devices, B)
    carry_shape = arr(8, B)
    parts = [BLOCK] * 4

    (pack,) = call(pack_kernel, "pack", [SM, SM, VM, VM], [arr(PACK, B)])(sector_shift, block_rows, psi, left)
    pack_low, pack_high = from_neighbours(pack)
    left2, right2, right_diag = call(
        split_kernel, "split", [SM, SM, SM, VM, VM],
        [arr(TERMS, B, 2 * B, dtype=bf16), arr(TERMS, LOCAL, B, 2 * B, dtype=bf16), arr(LOCAL, 8, B)],
    )(group, block_rows, weights, left, right_env)

    state3, diag3, *out = call(
        first_kernel, "first", [SM] * 3 + [VM] * 6, [BLOCK3, BLOCK3] + parts, SCRATCH
    )(group, sector_shift, weights, pack, pack_low, pack_high, left2, right2, right_diag)
    got = reduce_pair(out)
    image, stats = call(
        first_stats_kernel, "first_stats", [VM] * 4 + middle(1), [BLOCK, stats_shape]
    )(out[0], *got, state3)
    image_low, image_high = from_neighbours(image)
    stats = exchange(stats, devices)

    corr3, carry, *out = call(
        lambda *refs: start_kernel(count, *refs), "start", [SM] * 3 + [VM] * 8, [BLOCK3, carry_shape] + parts, SCRATCH
    )(group, sector_shift, weights, stats, state3, diag3, image, image_low, image_high, left2, right2)
    images = (image_low, image, image_high)
    image_own, own_spec = image.reshape(1, LOCAL, B, B), [pl.BlockSpec((1, LOCAL, B, B), lambda i: (0, 0, 0, 0))]

    for step in range(ITERS):
        got = reduce_pair(out)
        image_corr, stats = call(
            stats_kernel, "stats", [VM] * 4 + middle(2) + own_spec, [BLOCK, stats_shape]
        )(out[0], *got, state3, corr3, image_own)
        if step == ITERS - 1:
            break
        low, high = from_neighbours(image_corr)
        stats = exchange(stats, devices)
        if step == 0:
            im_specs, im_args = [VM] * 3, images
        else:
            im_specs = [pl.BlockSpec((None, LOCAL, B, B), lambda i, j=j: (j, 0, 0, 0)) for j in range(3)]
            im_args = (image3, image3, image3)
        state3, image3, corr3, carry, *out = call(
            lambda *refs, step=step: next_kernel(count, step, *refs), "next",
            [SM] * 3 + [VM] * 5 + im_specs + [VM] * 5, [BLOCK3] * 3 + [carry_shape] + parts, SCRATCH,
        )(group, sector_shift, weights, stats, carry, state3, diag3, corr3, *im_args, low, image_corr, high,
          left2, right2)
        image_own, own_spec = image3, middle(1)

    stats = exchange(stats, devices)
    state, energies = call(
        lambda *refs: last_kernel(count, *refs), "last", [VM] * 2 + middle(2), [BLOCK, arr(1, B)]
    )(stats, carry, state3, corr3)
    return state.reshape(psi_start.shape), energies[0, :ITERS]


def solution(mesh):
    in_specs = (
        P("sec", "pair", None, None),
        P(None, "sec", None, None),
        P(None, "pair", None, None),
        P(),
        P(),
        P(),
        P("sec"),
    )
    out_specs = (P("sec", "pair", None, None), P())
    return jax.shard_map(
        on_device, mesh=mesh, in_specs=in_specs, out_specs=out_specs, check_vma=False
    )
```

```python
import jax
import jax.numpy as jnp
from jax import lax
from jax.experimental import pallas as pl
from jax.experimental.pallas import tpu as pltpu
from jax.sharding import PartitionSpec as P

ITERS = 4
TERMS = 6
LOCAL = 4
GROUPS = 4
B = 128

f32 = jnp.float32
bf16 = jnp.bfloat16
VM = pl.BlockSpec(memory_space=pltpu.VMEM)
SM = pl.BlockSpec(memory_space=pltpu.SMEM)
PARAMS = pltpu.CompilerParams(vmem_limit_bytes=48 * 1024 * 1024)


def halves(x):
    high = x.astype(bf16)
    return high, (x - high.astype(f32)).astype(bf16)


def eye_mask():
    return lax.broadcasted_iota(jnp.int32, (B, B), 0) == lax.broadcasted_iota(jnp.int32, (B, B), 1)


def row_mask(rows):
    return (lax.broadcasted_iota(jnp.int32, (B, B), 0) < rows[0]).astype(f32)


def mask_kernel(rows, psi, state):
    keep = row_mask(rows)
    for p in range(LOCAL):
        state[p] = psi[p] * keep


def split_kernel(group, shift, rows, weights, left, right, left2, right2, diag):
    keep = row_mask(rows)
    eye = eye_mask()
    left_lines = []
    for k in range(TERMS):
        block = left[k] * keep
        left2[k] = jnp.concatenate(halves(block), axis=1)
        chosen = jnp.where(shift[k] == 0, 1.0, 0.0).astype(f32)
        left_lines.append(jnp.sum(jnp.where(eye, block, 0.0), axis=0, keepdims=True) * chosen)
    pad = jnp.zeros((8 - TERMS, B), f32)
    left_lines = jnp.concatenate(left_lines + [pad], axis=0)
    for q in range(LOCAL):
        lines = []
        for k in range(TERMS):
            block = right[k, q]
            right2[k, q] = jnp.concatenate(halves(jnp.transpose(block)), axis=1)
            p = group[0] * LOCAL + q
            scale = weights[k * 256 + p * 16 + p]
            lines.append(jnp.sum(jnp.where(eye, block, 0.0), axis=0, keepdims=True) * scale)
        diag[q] = lax.dot_general(
            left_lines, jnp.concatenate(lines + [pad], axis=0), (((0,), (0,)), ((), ())),
            precision=lax.Precision.HIGHEST, preferred_element_type=f32)


def mix(group, weights, z, out, target):
    for half in range(2):
        first = target * LOCAL + 2 * half
        acc = [None, None]
        for k in range(TERMS):
            for q in range(LOCAL):
                block = z[k * LOCAL + q]
                for j in range(2):
                    at = k * 256 + (first + j) * 16 + group[0] * LOCAL + q
                    part = weights[at] * block
                    acc[j] = part if acc[j] is None else acc[j] + part
        for j in range(2):
            out[2 * half + j] = acc[j]


def terms_kernel(group, sector, shift, weights, own, by_chip, by_core, left2, right2, z, out, vec2):
    odd = lax.rem(sector[0], 2)
    for p in range(LOCAL):
        vec2[1, p] = jnp.concatenate(halves(own[p]), axis=1)
        vec2[2 - 2 * odd, p] = jnp.concatenate(halves(by_core[p]), axis=1)
        vec2[2 * odd, p] = jnp.concatenate(halves(by_chip[p]), axis=1)
    for k in range(TERMS):
        source = shift[k] + 1
        lhs = left2[k]
        for q in range(LOCAL):
            r = right2[k, q]
            x = jnp.dot(vec2[source, q], jnp.concatenate([r, r], axis=0), preferred_element_type=f32)
            xh, xl = halves(x[:, :B] + x[:, B:])
            both = jnp.concatenate([xh, xl], axis=1)
            y = jnp.dot(lhs, jnp.concatenate([both, both], axis=0), preferred_element_type=f32)
            z[k * LOCAL + q] = y[:, :B] + y[:, B:]
    mix(group, weights, z, out, group[0] ^ 2)


def near_kernel(group, weights, z, out1, out3):
    mix(group, weights, z, out1, group[0] ^ 1)
    mix(group, weights, z, out3, group[0] ^ 3)


def own_kernel(group, weights, z, out):
    mix(group, weights, z, out, group[0])


def lane(row, j):
    at = lax.broadcasted_iota(jnp.int32, row.shape, 1) == j
    return jnp.sum(jnp.where(at, row, 0.0), axis=1, keepdims=True)


def put_lanes(values):
    at = lax.broadcasted_iota(jnp.int32, (1, B), 1)
    row = jnp.zeros((1, B), f32)
    for j, v in enumerate(values):
        row = jnp.where(at == j, v, row)
    return row


def lowest_root(lead, middle, const):
    root = jnp.sqrt(middle * middle - 4.0 * lead * const)
    return jnp.where(middle > 0, (-middle - root) / (2.0 * lead), 2.0 * const / (root - middle))


def ritz(sums, rayleigh, length):
    s_ic, c_i, curvature, correlation, spread = sums
    cross = 0.5 * (s_ic + c_i)
    lead = length * spread - correlation * correlation
    middle = -(length * curvature + spread * rayleigh - 2.0 * correlation * cross)
    const = rayleigh * curvature - cross * cross
    lowest = lowest_root(lead, middle, const)
    keep = curvature - lowest * spread
    add = lowest * correlation - cross
    norm = keep * keep * length + 2.0 * keep * add * correlation + add * add * spread
    factor = 1.0 / jnp.sqrt(norm)
    keep, add = keep * factor, add * factor
    rayleigh = keep * keep * rayleigh + 2.0 * keep * add * cross + add * add * curvature
    length = keep * keep * length + 2.0 * keep * add * correlation + add * add * spread
    return lowest, keep, add, rayleigh, length


def totals(stats, count, n):
    row = jnp.sum(stats[...], axis=0, keepdims=True) * (1.0 / count)
    return [lane(row, j) for j in range(n)]


def correct(state, image, diag, theta):
    return (image - theta * state) / jnp.maximum(jnp.abs(diag - theta), 1.0)


def start_kernel(count, stats, state, image, diag, corr, carry):
    rayleigh, length = totals(stats, count, 2)
    theta = rayleigh / length
    for p in range(LOCAL):
        corr[p] = correct(state[p], image[p], diag[p], theta)
    carry[...] = jnp.broadcast_to(put_lanes([rayleigh, length]), (8, B))


def next_kernel(count, step, stats, carry_in, state, image, diag, corr, more, state_out, image_out, corr_out, carry):
    sums = totals(stats, count, 5)
    old = carry_in[0:1, :]
    lowest, keep, add, rayleigh, length = ritz(sums, lane(old, 0), lane(old, 1))
    theta = rayleigh / length
    for p in range(LOCAL):
        s = keep * state[p] + add * corr[p]
        i = keep * image[p] + add * more[p]
        state_out[p] = s
        image_out[p] = i
        corr_out[p] = correct(s, i, diag[p], theta)
    energies = [lane(old, 2 + j) for j in range(step)] + [lowest]
    carry[...] = jnp.broadcast_to(put_lanes([rayleigh, length] + energies), (8, B))


def last_kernel(count, stats, carry_in, state, corr, state_out, energies):
    sums = totals(stats, count, 5)
    old = carry_in[0:1, :]
    lowest, keep, add, _, _ = ritz(sums, lane(old, 0), lane(old, 1))
    for p in range(LOCAL):
        state_out[p] = keep * state[p] + add * corr[p]
    for j, v in enumerate([lane(old, 2 + j) for j in range(ITERS - 1)] + [lowest]):
        energies[j] = v[0, 0]


def sum_all(block):
    return jnp.sum(jnp.sum(block, axis=0, keepdims=True), axis=1, keepdims=True)


def first_stats_kernel(own, r1, r2, r3, state, image, stats):
    a, b = jnp.zeros((B, B), f32), jnp.zeros((B, B), f32)
    for p in range(LOCAL):
        i = (own[p] + r2[p]) + (r1[p] + r3[p])
        s = state[p]
        image[p] = i
        a = a + s * i
        b = b + s * s
    stats[...] = jnp.broadcast_to(put_lanes([sum_all(a), sum_all(b)]), stats.shape)


def stats_kernel(own, r1, r2, r3, state, corr, image, image_corr, stats):
    acc = [jnp.zeros((B, B), f32) for _ in range(5)]
    for p in range(LOCAL):
        ic = (own[p] + r2[p]) + (r1[p] + r3[p])
        s, c, i = state[p], corr[p], image[p]
        image_corr[p] = ic
        for j, v in enumerate((s * ic, c * i, c * ic, s * c, c * c)):
            acc[j] = acc[j] + v
    stats[...] = jnp.broadcast_to(put_lanes([sum_all(a) for a in acc]), stats.shape)


def arr(*shape, dtype=f32):
    return jax.ShapeDtypeStruct(shape, dtype)


BLOCK = arr(LOCAL, B, B)
TERM_BLOCKS = arr(TERMS * LOCAL, B, B)


def call(kernel, name, in_specs, outs, scratch=(), out_specs=None, flops=0):
    moved = sum(o.size * o.dtype.itemsize for o in outs)
    return pl.pallas_call(
        kernel,
        out_shape=outs,
        in_specs=in_specs,
        out_specs=out_specs or [VM] * len(outs),
        scratch_shapes=list(scratch),
        compiler_params=PARAMS,
        cost_estimate=pl.CostEstimate(flops=flops, bytes_accessed=2 * moved, transcendentals=0),
        name=name,
    )


def swap(x, step):
    return lax.ppermute(x, "pair", [(i, i ^ step) for i in range(GROUPS)])


def neighbours(x):
    n = lax.axis_size("sec")
    by_chip = lax.ppermute(x, "sec", [(i, i + 1 if i % 2 else i - 1) for i in range(1, n - 1)])
    by_core = lax.ppermute(x, "sec", [(i, i ^ 1) for i in range(n)])
    return by_chip, by_core


def exchange(stats, devices):
    got = lax.all_to_all(stats.reshape(devices, 1, B), ("sec", "pair"), 0, 0)
    return got.reshape(devices, B)


def on_device(psi_start, left_env, right_env, mpo_coef, mpo_pattern, sector_shift, block_rows):
    devices = lax.axis_size("sec") * lax.axis_size("pair")
    count = float(psi_start.size * devices)
    psi = psi_start.reshape(LOCAL, B, B)
    left = left_env.reshape(TERMS, B, B)
    group = lax.axis_index("pair").astype(jnp.int32).reshape(1)
    sector = lax.axis_index("sec").astype(jnp.int32).reshape(1)
    weights = (mpo_coef * mpo_pattern.astype(f32)).reshape(-1)
    stats_shape = arr(devices, B)
    carry_shape = arr(8, B)

    def shares(vector, near, left2, right2):
        by_chip, by_core = near
        z, part2 = call(
            terms_kernel, "terms", [SM] * 4 + [VM] * 5, [TERM_BLOCKS, BLOCK],
            [pltpu.VMEM((3, LOCAL, B, 2 * B), bf16)],
        )(group, sector, sector_shift, weights, vector, by_chip, by_core, left2, right2)
        got2 = swap(part2, 2)
        part1, part3 = call(near_kernel, "near", [SM, SM, VM], [BLOCK] * 2)(group, weights, z)
        got1, got3 = swap(part1, 1), swap(part3, 3)
        (own,) = call(own_kernel, "own", [SM, SM, VM], [BLOCK])(group, weights, z)
        return own, got1, got2, got3

    (state,) = call(mask_kernel, "mask", [SM, VM], [BLOCK])(block_rows, psi)
    near = neighbours(state)
    left2, right2, diag = call(
        split_kernel, "split", [SM] * 4 + [VM] * 2,
        [arr(TERMS, B, 2 * B, dtype=bf16), arr(TERMS, LOCAL, B, 2 * B, dtype=bf16), BLOCK],
    )(group, sector_shift, block_rows, weights, left, right_env)

    image, stats = call(first_stats_kernel, "first_stats", [VM] * 5, [BLOCK, stats_shape])(
        *shares(state, near, left2, right2), state)
    stats = exchange(stats, devices)
    corr, carry = call(
        lambda *refs: start_kernel(count, *refs), "start", [VM] * 4, [BLOCK, carry_shape]
    )(stats, state, image, diag)

    for step in range(ITERS):
        image_corr, stats = call(stats_kernel, "stats", [VM] * 7, [BLOCK, stats_shape])(
            *shares(corr, neighbours(corr), left2, right2), state, corr, image)
        stats = exchange(stats, devices)
        if step < ITERS - 1:
            state, image, corr, carry = call(
                lambda *refs, step=step: next_kernel(count, step, *refs), "next", [VM] * 7, [BLOCK] * 3 + [carry_shape]
            )(stats, carry, state, image, diag, corr, image_corr)

    state, energies = call(
        lambda *refs: last_kernel(count, *refs), "last", [VM] * 4, [BLOCK, arr(ITERS)], out_specs=[VM, SM]
    )(stats, carry, state, corr)
    return state.reshape(psi_start.shape), energies


def solution(mesh):
    in_specs = (
        P("sec", "pair", None, None),
        P(None, "sec", None, None),
        P(None, "pair", None, None),
        P(),
        P(),
        P(),
        P("sec"),
    )
    out_specs = (P("sec", "pair", None, None), P())
    return jax.shard_map(
        on_device, mesh=mesh, in_specs=in_specs, out_specs=out_specs, check_vma=False
    )
```

```python
import jax
import jax.numpy as jnp
from jax import lax
from jax.experimental import pallas as pl
from jax.experimental.pallas import tpu as pltpu
from jax.sharding import PartitionSpec as P

ITERS = 4
ROWS = 1
TERMS = 6
LOCAL = 4
GROUPS = 4
B = 128
PACK = LOCAL * B + 8

f32 = jnp.float32
bf16 = jnp.bfloat16
VM = pl.BlockSpec(memory_space=pltpu.VMEM)
SM = pl.BlockSpec(memory_space=pltpu.SMEM)
ANY = pl.BlockSpec(memory_space=pl.ANY)
PARAMS = pltpu.CompilerParams(vmem_limit_bytes=24 * 1024 * 1024)


def halves(x):
    high = x.astype(bf16)
    return high, (x - high.astype(f32)).astype(bf16)


def eye_mask():
    return lax.broadcasted_iota(jnp.int32, (B, B), 0) == lax.broadcasted_iota(jnp.int32, (B, B), 1)


def row_mask(rows):
    return (lax.broadcasted_iota(jnp.int32, (B, B), 0) < rows[0]).astype(f32)


def mask_kernel(rows, psi, state):
    keep = row_mask(rows)
    for p in range(LOCAL):
        state[p] = psi[p] * keep


def outer(left_lines, right_lines):
    return lax.dot_general(
        left_lines, right_lines, (((0,), (0,)), ((), ())),
        precision=lax.Precision.HIGHEST, preferred_element_type=f32)


def split_kernel(group, shift, rows, weights, left, right, left2, right2, diag, left_diag, right_diag,
                 left_buf, right_buf, sems):
    copies = [pltpu.make_async_copy(left, left_buf, sems.at[TERMS])]
    copies += [pltpu.make_async_copy(right.at[k], right_buf.at[k], sems.at[k]) for k in range(TERMS)]
    for copy in copies:
        copy.start()
    keep = row_mask(rows)
    eye = eye_mask()
    pad = jnp.zeros((8 - TERMS, B), f32)
    lines = []
    copies[0].wait()
    for k in range(TERMS):
        block = left_buf[k] * keep
        left2[k] = jnp.concatenate(halves(block), axis=1)
        chosen = jnp.where(shift[k] == 0, 1.0, 0.0).astype(f32)
        lines.append(jnp.sum(jnp.where(eye, block, 0.0), axis=0, keepdims=True) * chosen)
    left_diag[...] = jnp.concatenate(lines + [pad], axis=0)
    lines = [[] for _ in range(LOCAL)]
    for k in range(TERMS):
        copies[1 + k].wait()
        for q in range(LOCAL):
            block = right_buf[k, q]
            right2[k, q] = jnp.concatenate(halves(jnp.transpose(block)), axis=1)
            p = group[0] * LOCAL + q
            scale = weights[k * 256 + p * 16 + p]
            lines[q].append(jnp.sum(jnp.where(eye, block, 0.0), axis=0, keepdims=True) * scale)
    for q in range(LOCAL):
        right_diag[q] = jnp.concatenate(lines[q] + [pad], axis=0)
        diag[q] = outer(left_diag[...], right_diag[q])


def mix(group, weights, z, out, target, at_out=0):
    for half in range(2):
        first = target * LOCAL + 2 * half
        acc = [None, None]
        for k in range(TERMS):
            for q in range(LOCAL):
                block = z[k * LOCAL + q]
                for j in range(2):
                    at = k * 256 + (first + j) * 16 + group[0] * LOCAL + q
                    part = weights[at] * block
                    acc[j] = part if acc[j] is None else acc[j] + part
        for j in range(2):
            out[at_out + 2 * half + j] = acc[j]


def terms_kernel(group, sector, shift, weights, own, by_chip, by_core, left2, right2, z, out, vec2):
    odd = lax.rem(sector[0], 2)
    for p in range(LOCAL):
        vec2[1, p] = jnp.concatenate(halves(own[p]), axis=1)
        vec2[2 - 2 * odd, p] = jnp.concatenate(halves(by_core[p]), axis=1)
        vec2[2 * odd, p] = jnp.concatenate(halves(by_chip[p]), axis=1)
    for k in range(TERMS):
        source = shift[k] + 1
        lhs = left2[k]
        for q in range(LOCAL):
            r = right2[k, q]
            x = jnp.dot(vec2[source, q], jnp.concatenate([r, r], axis=0), preferred_element_type=f32)
            xh, xl = halves(x[:, :B] + x[:, B:])
            both = jnp.concatenate([xh, xl], axis=1)
            y = jnp.dot(lhs, jnp.concatenate([both, both], axis=0), preferred_element_type=f32)
            z[k * LOCAL + q] = y[:, :B] + y[:, B:]
    mix(group, weights, z, out, group[0] ^ (1 + 2 * odd))
    mix(group, weights, z, out, group[0] ^ 2, LOCAL)


def rest_kernel(group, sector, weights, z, own, onward):
    odd = lax.rem(sector[0], 2)
    mix(group, weights, z, own, group[0])
    mix(group, weights, z, onward, group[0] ^ (3 - 2 * odd))


def onward_kernel(onward, first, out):
    for p in range(LOCAL):
        out[p] = onward[p] + first[LOCAL + p]


def lane(row, j):
    at = lax.broadcasted_iota(jnp.int32, row.shape, 1) == j
    return jnp.sum(jnp.where(at, row, 0.0), axis=1, keepdims=True)


def put_lanes(values):
    at = lax.broadcasted_iota(jnp.int32, (1, B), 1)
    row = jnp.zeros((1, B), f32)
    for j, v in enumerate(values):
        row = jnp.where(at == j, v, row)
    return row


def lowest_root(lead, middle, const):
    root = jnp.sqrt(middle * middle - 4.0 * lead * const)
    return jnp.where(middle > 0, (-middle - root) / (2.0 * lead), 2.0 * const / (root - middle))


def ritz(sums, rayleigh, length):
    s_ic, c_i, curvature, correlation, spread = sums
    cross = 0.5 * (s_ic + c_i)
    lead = length * spread - correlation * correlation
    middle = -(length * curvature + spread * rayleigh - 2.0 * correlation * cross)
    const = rayleigh * curvature - cross * cross
    lowest = lowest_root(lead, middle, const)
    keep = curvature - lowest * spread
    add = lowest * correlation - cross
    norm = keep * keep * length + 2.0 * keep * add * correlation + add * add * spread
    factor = 1.0 / jnp.sqrt(norm)
    keep, add = keep * factor, add * factor
    rayleigh = keep * keep * rayleigh + 2.0 * keep * add * cross + add * add * curvature
    length = keep * keep * length + 2.0 * keep * add * correlation + add * add * spread
    return lowest, keep, add, rayleigh, length


def totals(stats, count, n):
    row = jnp.sum(stats[...], axis=0, keepdims=True) * (1.0 / (ROWS * count))
    return [lane(row, j) for j in range(n)]


def correct(state, image, diag, theta):
    return (image - theta * state) / jnp.maximum(jnp.abs(diag - theta), 1.0)


def start_kernel(count, stats, s0, s1, s2, pack0, pack1, pack2, diag0, right_diag,
                 i0, i1, i2, diag1, diag2, c0, c1, c2, carry):
    rayleigh, length = totals(stats, count, 2)
    theta = rayleigh / length
    for pack, diag in ((pack1, diag1), (pack2, diag2)):
        for p in range(LOCAL):
            diag[p] = outer(pack[LOCAL * B:PACK, :], right_diag[p])
    for s, pack, i, diag, c in ((s0, pack0, i0, diag0, c0), (s1, pack1, i1, diag1, c1), (s2, pack2, i2, diag2, c2)):
        for p in range(LOCAL):
            block = pack[p * B:(p + 1) * B, :]
            i[p] = block
            c[p] = correct(s[p], block, diag[p], theta)
    carry[...] = jnp.broadcast_to(put_lanes([rayleigh, length]), (8, B))


def next_kernel(count, step, stats, carry_in, *refs):
    sums = totals(stats, count, 5)
    old = carry_in[0:1, :]
    lowest, keep, add, rayleigh, length = ritz(sums, lane(old, 0), lane(old, 1))
    theta = rayleigh / length
    for n in range(3):
        state, image, corr, diag, more, state_out, image_out, corr_out = refs[n:24:3]
        for p in range(LOCAL):
            s = keep * state[p] + add * corr[p]
            i = keep * image[p] + add * more[p]
            state_out[p] = s
            image_out[p] = i
            corr_out[p] = correct(s, i, diag[p], theta)
    energies = [lane(old, 2 + j) for j in range(step)] + [lowest]
    refs[24][...] = jnp.broadcast_to(put_lanes([rayleigh, length] + energies), (8, B))


def last_kernel(count, stats, carry_in, state, corr, state_out, energies):
    sums = totals(stats, count, 5)
    old = carry_in[0:1, :]
    lowest, keep, add, _, _ = ritz(sums, lane(old, 0), lane(old, 1))
    for p in range(LOCAL):
        state_out[p] = keep * state[p] + add * corr[p]
    for j, v in enumerate([lane(old, 2 + j) for j in range(ITERS - 1)] + [lowest]):
        energies[j] = v[0, 0]


def sum_all(block):
    return jnp.sum(jnp.sum(block, axis=0, keepdims=True), axis=1, keepdims=True)


def first_stats_kernel(own, first, second, state, stats):
    a, b = jnp.zeros((B, B), f32), jnp.zeros((B, B), f32)
    for p in range(LOCAL):
        i = (own[p] + first[p]) + second[p]
        s = state[p]
        a = a + s * i
        b = b + s * s
    stats[...] = jnp.broadcast_to(put_lanes([sum_all(a), sum_all(b)]), stats.shape)


def first_sum_kernel(own, first, second, left_diag, stats, pack):
    for p in range(LOCAL):
        pack[p * B:(p + 1) * B, :] = (own[p] + first[p]) + second[p]
    pack[LOCAL * B:PACK, :] = left_diag[...]


def stats_kernel(own, first, second, state, corr, image, stats):
    acc = [jnp.zeros((B, B), f32) for _ in range(5)]
    for p in range(LOCAL):
        ic = (own[p] + first[p]) + second[p]
        s, c, i = state[p], corr[p], image[p]
        for j, v in enumerate((s * ic, c * i, c * ic, s * c, c * c)):
            acc[j] = acc[j] + v
    stats[...] = jnp.broadcast_to(put_lanes([sum_all(a) for a in acc]), stats.shape)


def sum_kernel(own, first, second, stats, image_corr):
    for p in range(LOCAL):
        image_corr[p] = (own[p] + first[p]) + second[p]


def arr(*shape, dtype=f32):
    return jax.ShapeDtypeStruct(shape, dtype)


BLOCK = arr(LOCAL, B, B)
TERM_BLOCKS = arr(TERMS * LOCAL, B, B)


def call(kernel, name, in_specs, outs, scratch=(), out_specs=None, flops=0):
    moved = sum(o.size * o.dtype.itemsize for o in outs)
    return pl.pallas_call(
        kernel,
        out_shape=outs,
        in_specs=in_specs,
        out_specs=out_specs or [VM] * len(outs),
        scratch_shapes=list(scratch),
        compiler_params=PARAMS,
        cost_estimate=pl.CostEstimate(flops=flops, bytes_accessed=2 * moved, transcendentals=0),
        name=name,
    )


def swap(x, even, odd):
    n = lax.axis_size("sec")
    perm = [(s * GROUPS + g, s * GROUPS + (g ^ (odd if s % 2 else even))) for s in range(n) for g in range(GROUPS)]
    return lax.ppermute(x, ("sec", "pair"), perm)


def neighbours(x):
    n = lax.axis_size("sec")
    by_chip = lax.ppermute(x, "sec", [(i, i + 1 if i % 2 else i - 1) for i in range(1, n - 1)])
    by_core = lax.ppermute(x, "sec", [(i, i ^ 1) for i in range(n)])
    return by_chip, by_core


def exchange(stats, devices):
    got = lax.all_to_all(stats.reshape(devices, ROWS, B), ("sec", "pair"), 0, 0)
    return got.reshape(ROWS * devices, B)


def on_device(psi_start, left_env, right_env, mpo_coef, mpo_pattern, sector_shift, block_rows):
    devices = lax.axis_size("sec") * lax.axis_size("pair")
    count = float(psi_start.size * devices)
    psi = psi_start.reshape(LOCAL, B, B)
    left = left_env.reshape(TERMS, B, B)
    group = lax.axis_index("pair").astype(jnp.int32).reshape(1)
    sector = lax.axis_index("sec").astype(jnp.int32).reshape(1)
    weights = (mpo_coef * mpo_pattern.astype(f32)).reshape(-1)
    stats_shape = arr(ROWS * devices, B)
    carry_shape = arr(8, B)

    def shares(vectors, left2, right2):
        z, part = call(
            terms_kernel, "terms", [SM] * 4 + [VM] * 5, [TERM_BLOCKS, arr(2 * LOCAL, B, B)],
            [pltpu.VMEM((3, LOCAL, B, 2 * B), bf16)],
        )(group, sector, sector_shift, weights, *vectors, left2, right2)
        first = swap(part, 1, 3)
        own, onward = call(rest_kernel, "rest", [SM] * 3 + [VM], [BLOCK] * 2)(group, sector, weights, z)
        (onward,) = call(onward_kernel, "onward", [VM] * 2, [BLOCK])(onward, first)
        return own, first, swap(onward, 3, 1)

    (state,) = call(mask_kernel, "mask", [SM, VM], [BLOCK])(block_rows, psi)
    states = (state, *neighbours(state))
    left2, right2, diag, left_diag, right_diag = call(
        split_kernel, "split", [SM] * 4 + [ANY] * 2,
        [arr(TERMS, B, 2 * B, dtype=bf16), arr(TERMS, LOCAL, B, 2 * B, dtype=bf16), BLOCK, arr(8, B), arr(LOCAL, 8, B)],
        [pltpu.VMEM((TERMS, B, B), f32), pltpu.VMEM((TERMS, LOCAL, B, B), f32), pltpu.SemaphoreType.DMA((TERMS + 1,))],
    )(group, sector_shift, block_rows, weights, left, right_env)

    parts = shares(states, left2, right2)
    (stats,) = call(first_stats_kernel, "first_stats", [VM] * 4, [stats_shape])(*parts, state)
    (pack,) = call(first_sum_kernel, "first_sum", [VM] * 4 + [ANY], [arr(PACK, B)])(*parts, left_diag, stats)
    packs = (pack, *neighbours(pack))
    *out, carry = call(
        lambda *refs: start_kernel(count, *refs), "start", [VM] * 9, [BLOCK] * 8 + [carry_shape]
    )(exchange(stats, devices), *states, *packs, diag, right_diag)
    images, diags, corrs = out[:3], (diag, *out[3:5]), out[5:8]

    for step in range(ITERS):
        parts = shares(corrs, left2, right2)
        (stats,) = call(stats_kernel, "stats", [VM] * 6, [stats_shape])(*parts, states[0], corrs[0], images[0])
        got = exchange(stats, devices)
        if step < ITERS - 1:
            (image_corr,) = call(sum_kernel, "sum", [VM] * 3 + [ANY], [BLOCK])(*parts, stats)
            more = (image_corr, *neighbours(image_corr))
            *out, carry = call(
                lambda *refs, step=step: next_kernel(count, step, *refs), "next", [VM] * 17, [BLOCK] * 9 + [carry_shape]
            )(got, carry, *states, *images, *corrs, *diags, *more)
            states, images, corrs = out[:3], out[3:6], out[6:9]

    state, energies = call(
        lambda *refs: last_kernel(count, *refs), "last", [VM] * 4, [BLOCK, arr(ITERS)], out_specs=[VM, SM]
    )(got, carry, states[0], corrs[0])
    return state.reshape(psi_start.shape), energies


def solution(mesh):
    in_specs = (
        P("sec", "pair", None, None),
        P(None, "sec", None, None),
        P(None, "pair", None, None),
        P(),
        P(),
        P(),
        P("sec"),
    )
    out_specs = (P("sec", "pair", None, None), P())
    return jax.shard_map(
        on_device, mesh=mesh, in_specs=in_specs, out_specs=out_specs, check_vma=False
    )
```

```python
import jax
import jax.numpy as jnp
from jax import lax
from jax.experimental import pallas as pl
from jax.experimental.pallas import tpu as pltpu
from jax.sharding import PartitionSpec as P

ITERS = 4
TERMS = 6
LOCAL = 4
GROUPS = 4
B = 128
PACK = LOCAL * B + 8

f32 = jnp.float32
bf16 = jnp.bfloat16
VM = pl.BlockSpec(memory_space=pltpu.VMEM)
SM = pl.BlockSpec(memory_space=pltpu.SMEM)
PARAMS = pltpu.CompilerParams(vmem_limit_bytes=24 * 1024 * 1024)


def halves(x):
    high = x.astype(bf16)
    return high, (x - high.astype(f32)).astype(bf16)


def eye_mask():
    return lax.broadcasted_iota(jnp.int32, (B, B), 0) == lax.broadcasted_iota(jnp.int32, (B, B), 1)


def row_mask(rows):
    return (lax.broadcasted_iota(jnp.int32, (B, B), 0) < rows[0]).astype(f32)


def mask_kernel(rows, psi, state):
    keep = row_mask(rows)
    for p in range(LOCAL):
        state[p] = psi[p] * keep


def outer(left_lines, right_lines):
    return lax.dot_general(
        left_lines, right_lines, (((0,), (0,)), ((), ())),
        precision=lax.Precision.HIGHEST, preferred_element_type=f32)


def split_kernel(group, shift, rows, weights, left, right, left2, right2, diag, left_diag, right_diag):
    keep = row_mask(rows)
    eye = eye_mask()
    pad = jnp.zeros((8 - TERMS, B), f32)
    lines = []
    for k in range(TERMS):
        block = left[k] * keep
        left2[k] = jnp.concatenate(halves(block), axis=1)
        chosen = jnp.where(shift[k] == 0, 1.0, 0.0).astype(f32)
        lines.append(jnp.sum(jnp.where(eye, block, 0.0), axis=0, keepdims=True) * chosen)
    left_diag[...] = jnp.concatenate(lines + [pad], axis=0)
    lines = [[] for _ in range(LOCAL)]
    for k in range(TERMS):
        for q in range(LOCAL):
            block = right[k, q]
            right2[k, q] = jnp.concatenate(halves(jnp.transpose(block)), axis=1)
            p = group[0] * LOCAL + q
            scale = weights[k * 256 + p * 16 + p]
            lines[q].append(jnp.sum(jnp.where(eye, block, 0.0), axis=0, keepdims=True) * scale)
    for q in range(LOCAL):
        right_diag[q] = jnp.concatenate(lines[q] + [pad], axis=0)
        diag[q] = outer(left_diag[...], right_diag[q])


def mix(group, weights, z, target, outs):
    for half, (out, at_out) in enumerate(outs):
        first = target * LOCAL + 2 * half
        acc = [None, None]
        for k in range(TERMS):
            for q in range(LOCAL):
                block = z[k * LOCAL + q]
                for j in range(2):
                    at = k * 256 + (first + j) * 16 + group[0] * LOCAL + q
                    part = weights[at] * block
                    acc[j] = part if acc[j] is None else acc[j] + part
        for j in range(2):
            out[at_out + j] = acc[j]


def terms_kernel(group, sector, shift, weights, own, by_chip, by_core, left2, right2, z, far1, far3, vec2):
    odd = lax.rem(sector[0], 2)
    for p in range(LOCAL):
        vec2[1, p] = jnp.concatenate(halves(own[p]), axis=1)
        vec2[2 - 2 * odd, p] = jnp.concatenate(halves(by_core[p]), axis=1)
        vec2[2 * odd, p] = jnp.concatenate(halves(by_chip[p]), axis=1)
    for k in range(TERMS):
        source = shift[k] + 1
        lhs = left2[k]
        for q in range(LOCAL):
            r = right2[k, q]
            x = jnp.dot(vec2[source, q], jnp.concatenate([r, r], axis=0), preferred_element_type=f32)
            xh, xl = halves(x[:, :B] + x[:, B:])
            both = jnp.concatenate([xh, xl], axis=1)
            y = jnp.dot(lhs, jnp.concatenate([both, both], axis=0), preferred_element_type=f32)
            z[k * LOCAL + q] = y[:, :B] + y[:, B:]
    mix(group, weights, z, group[0] ^ 2, ((far1, 0), (far3, 0)))


def near_kernel(group, weights, z, near1, near3):
    mix(group, weights, z, group[0] ^ 1, ((near1, 0), (near1, 2)))
    mix(group, weights, z, group[0] ^ 3, ((near3, 0), (near3, 2)))


def relay_kernel(near1, near3, got1, got3, out1, out3):
    for j in range(2):
        out1[j] = near1[j]
        out1[2 + j] = near1[2 + j] + got3[j]
        out3[j] = near3[j] + got1[j]
        out3[2 + j] = near3[2 + j]


def own_kernel(group, weights, z, own):
    mix(group, weights, z, group[0], ((own, 0), (own, 2)))


def lane(row, j):
    at = lax.broadcasted_iota(jnp.int32, row.shape, 1) == j
    return jnp.sum(jnp.where(at, row, 0.0), axis=1, keepdims=True)


def put_lanes(values):
    at = lax.broadcasted_iota(jnp.int32, (1, B), 1)
    row = jnp.zeros((1, B), f32)
    for j, v in enumerate(values):
        row = jnp.where(at == j, v, row)
    return row


def lowest_root(lead, middle, const):
    root = jnp.sqrt(middle * middle - 4.0 * lead * const)
    return jnp.where(middle > 0, (-middle - root) / (2.0 * lead), 2.0 * const / (root - middle))


def ritz(sums, rayleigh, length):
    s_ic, c_i, curvature, correlation, spread = sums
    cross = 0.5 * (s_ic + c_i)
    lead = length * spread - correlation * correlation
    middle = -(length * curvature + spread * rayleigh - 2.0 * correlation * cross)
    const = rayleigh * curvature - cross * cross
    lowest = lowest_root(lead, middle, const)
    keep = curvature - lowest * spread
    add = lowest * correlation - cross
    norm = keep * keep * length + 2.0 * keep * add * correlation + add * add * spread
    factor = 1.0 / jnp.sqrt(norm)
    keep, add = keep * factor, add * factor
    rayleigh = keep * keep * rayleigh + 2.0 * keep * add * cross + add * add * curvature
    length = keep * keep * length + 2.0 * keep * add * correlation + add * add * spread
    return lowest, keep, add, rayleigh, length


def totals(stats, count, n):
    row = jnp.sum(stats[...], axis=0, keepdims=True) * (1.0 / count)
    return [lane(row, j) for j in range(n)]


def correct(state, image, diag, theta):
    return (image - theta * state) / jnp.maximum(jnp.abs(diag - theta), 1.0)


def start_kernel(count, stats, s0, s1, s2, pack0, pack1, pack2, diag0, right_diag,
                 i0, i1, i2, diag1, diag2, c0, c1, c2, carry):
    rayleigh, length = totals(stats, count, 2)
    theta = rayleigh / length
    for pack, diag in ((pack1, diag1), (pack2, diag2)):
        for p in range(LOCAL):
            diag[p] = outer(pack[LOCAL * B:PACK, :], right_diag[p])
    for s, pack, i, diag, c in ((s0, pack0, i0, diag0, c0), (s1, pack1, i1, diag1, c1), (s2, pack2, i2, diag2, c2)):
        for p in range(LOCAL):
            block = pack[p * B:(p + 1) * B, :]
            i[p] = block
            c[p] = correct(s[p], block, diag[p], theta)
    carry[...] = jnp.broadcast_to(put_lanes([rayleigh, length]), (8, B))


def next_kernel(count, step, stats, carry_in, *refs):
    sums = totals(stats, count, 5)
    old = carry_in[0:1, :]
    lowest, keep, add, rayleigh, length = ritz(sums, lane(old, 0), lane(old, 1))
    theta = rayleigh / length
    for n in range(3):
        state, image, corr, diag, more, state_out, image_out, corr_out = refs[n:24:3]
        for p in range(LOCAL):
            s = keep * state[p] + add * corr[p]
            i = keep * image[p] + add * more[p]
            state_out[p] = s
            image_out[p] = i
            corr_out[p] = correct(s, i, diag[p], theta)
    energies = [lane(old, 2 + j) for j in range(step)] + [lowest]
    refs[24][...] = jnp.broadcast_to(put_lanes([rayleigh, length] + energies), (8, B))


def last_kernel(count, stats, carry_in, state, corr, state_out, energies):
    sums = totals(stats, count, 5)
    old = carry_in[0:1, :]
    lowest, keep, add, _, _ = ritz(sums, lane(old, 0), lane(old, 1))
    for p in range(LOCAL):
        state_out[p] = keep * state[p] + add * corr[p]
    for j, v in enumerate([lane(old, 2 + j) for j in range(ITERS - 1)] + [lowest]):
        energies[j] = v[0, 0]


def sum_all(block):
    return jnp.sum(jnp.sum(block, axis=0, keepdims=True), axis=1, keepdims=True)


def first_stats_kernel(own, got1, got3, state, left_diag, pack, stats):
    a, b = jnp.zeros((B, B), f32), jnp.zeros((B, B), f32)
    for p in range(LOCAL):
        i = own[p] + (got1[p] + got3[p])
        s = state[p]
        pack[p * B:(p + 1) * B, :] = i
        a = a + s * i
        b = b + s * s
    pack[LOCAL * B:PACK, :] = left_diag[...]
    stats[...] = jnp.broadcast_to(put_lanes([sum_all(a), sum_all(b)]), stats.shape)


def stats_kernel(own, got1, got3, state, corr, image, image_corr, stats):
    acc = [jnp.zeros((B, B), f32) for _ in range(5)]
    for p in range(LOCAL):
        ic = own[p] + (got1[p] + got3[p])
        s, c, i = state[p], corr[p], image[p]
        image_corr[p] = ic
        for j, v in enumerate((s * ic, c * i, c * ic, s * c, c * c)):
            acc[j] = acc[j] + v
    stats[...] = jnp.broadcast_to(put_lanes([sum_all(a) for a in acc]), stats.shape)


def arr(*shape, dtype=f32):
    return jax.ShapeDtypeStruct(shape, dtype)


BLOCK = arr(LOCAL, B, B)
HALF = arr(LOCAL // 2, B, B)
TERM_BLOCKS = arr(TERMS * LOCAL, B, B)


def call(kernel, name, in_specs, outs, scratch=(), out_specs=None, flops=0):
    moved = sum(o.size * o.dtype.itemsize for o in outs)
    return pl.pallas_call(
        kernel,
        out_shape=outs,
        in_specs=in_specs,
        out_specs=out_specs or [VM] * len(outs),
        scratch_shapes=list(scratch),
        compiler_params=PARAMS,
        cost_estimate=pl.CostEstimate(flops=flops, bytes_accessed=2 * moved, transcendentals=0),
        name=name,
    )


def swap(x, step):
    return lax.ppermute(x, "pair", [(i, i ^ step) for i in range(GROUPS)])


def neighbours(x):
    n = lax.axis_size("sec")
    by_chip = lax.ppermute(x, "sec", [(i, i + 1 if i % 2 else i - 1) for i in range(1, n - 1)])
    by_core = lax.ppermute(x, "sec", [(i, i ^ 1) for i in range(n)])
    return by_chip, by_core


def exchange(stats, devices):
    got = lax.all_to_all(stats.reshape(devices, 1, B), ("sec", "pair"), 0, 0)
    return got.reshape(devices, B)


def on_device(psi_start, left_env, right_env, mpo_coef, mpo_pattern, sector_shift, block_rows):
    devices = lax.axis_size("sec") * lax.axis_size("pair")
    count = float(psi_start.size * devices)
    psi = psi_start.reshape(LOCAL, B, B)
    left = left_env.reshape(TERMS, B, B)
    group = lax.axis_index("pair").astype(jnp.int32).reshape(1)
    sector = lax.axis_index("sec").astype(jnp.int32).reshape(1)
    weights = (mpo_coef * mpo_pattern.astype(f32)).reshape(-1)
    stats_shape = arr(devices, B)
    carry_shape = arr(8, B)

    def shares(vectors, left2, right2):
        z, far1, far3 = call(
            terms_kernel, "terms", [SM] * 4 + [VM] * 5, [TERM_BLOCKS, HALF, HALF],
            [pltpu.VMEM((3, LOCAL, B, 2 * B), bf16)],
        )(group, sector, sector_shift, weights, *vectors, left2, right2)
        far1, far3 = swap(far1, 1), swap(far3, 3)
        near1, near3 = call(near_kernel, "near", [SM, SM, VM], [BLOCK] * 2)(group, weights, z)
        near1, near3 = call(relay_kernel, "relay", [VM] * 4, [BLOCK] * 2)(near1, near3, far1, far3)
        got1, got3 = swap(near1, 1), swap(near3, 3)
        (own,) = call(own_kernel, "own", [SM, SM, VM], [BLOCK])(group, weights, z)
        return own, got1, got3

    (state,) = call(mask_kernel, "mask", [SM, VM], [BLOCK])(block_rows, psi)
    states = (state, *neighbours(state))
    left2, right2, diag, left_diag, right_diag = call(
        split_kernel, "split", [SM] * 4 + [VM] * 2,
        [arr(TERMS, B, 2 * B, dtype=bf16), arr(TERMS, LOCAL, B, 2 * B, dtype=bf16), BLOCK, arr(8, B), arr(LOCAL, 8, B)],
    )(group, sector_shift, block_rows, weights, left, right_env)

    parts = shares(states, left2, right2)
    pack, stats = call(first_stats_kernel, "first_stats", [VM] * 5, [arr(PACK, B), stats_shape])(
        *parts, state, left_diag)
    packs = (pack, *neighbours(pack))
    *out, carry = call(
        lambda *refs: start_kernel(count, *refs), "start", [VM] * 9, [BLOCK] * 8 + [carry_shape]
    )(exchange(stats, devices), *states, *packs, diag, right_diag)
    images, diags, corrs = out[:3], (diag, *out[3:5]), out[5:8]

    for step in range(ITERS):
        parts = shares(corrs, left2, right2)
        image_corr, stats = call(stats_kernel, "stats", [VM] * 6, [BLOCK, stats_shape])(
            *parts, states[0], corrs[0], images[0])
        got = exchange(stats, devices)
        if step < ITERS - 1:
            more = (image_corr, *neighbours(image_corr))
            *out, carry = call(
                lambda *refs, step=step: next_kernel(count, step, *refs), "next", [VM] * 17, [BLOCK] * 9 + [carry_shape]
            )(got, carry, *states, *images, *corrs, *diags, *more)
            states, images, corrs = out[:3], out[3:6], out[6:9]

    state, energies = call(
        lambda *refs: last_kernel(count, *refs), "last", [VM] * 4, [BLOCK, arr(ITERS)], out_specs=[VM, SM]
    )(got, carry, states[0], corrs[0])
    return state.reshape(psi_start.shape), energies


def solution(mesh):
    in_specs = (
        P("sec", "pair", None, None),
        P(None, "sec", None, None),
        P(None, "pair", None, None),
        P(),
        P(),
        P(),
        P("sec"),
    )
    out_specs = (P("sec", "pair", None, None), P())
    return jax.shard_map(
        on_device, mesh=mesh, in_specs=in_specs, out_specs=out_specs, check_vma=False
    )
```

```python
import functools

import jax
import jax.numpy as jnp
from jax import lax
from jax.experimental import pallas as pl
from jax.experimental.pallas import tpu as pltpu
from jax.sharding import PartitionSpec as P

ITERS = 4
TERMS = 6
LOCAL = 4
GROUPS = 4
B = 128
PACK = LOCAL * B + 8

f32 = jnp.float32
bf16 = jnp.bfloat16
VM = pl.BlockSpec(memory_space=pltpu.VMEM)
SM = pl.BlockSpec(memory_space=pltpu.SMEM)
ANY = pl.BlockSpec(memory_space=pl.ANY)
PARAMS = pltpu.CompilerParams(vmem_limit_bytes=24 * 1024 * 1024)


def halves(x):
    high = x.astype(bf16)
    return high, (x - high.astype(f32)).astype(bf16)


def eye_mask():
    return lax.broadcasted_iota(jnp.int32, (B, B), 0) == lax.broadcasted_iota(jnp.int32, (B, B), 1)


def row_mask(rows):
    return (lax.broadcasted_iota(jnp.int32, (B, B), 0) < rows[0]).astype(f32)


def mask_kernel(rows, psi, state):
    keep = row_mask(rows)
    for p in range(LOCAL):
        state[p] = psi[p] * keep


def outer(left_lines, right_lines):
    return lax.dot_general(
        left_lines, right_lines, (((0,), (0,)), ((), ())),
        precision=lax.Precision.HIGHEST, preferred_element_type=f32)


def split_kernel(group, shift, rows, weights, left, right, left2, right2, diag, left_diag, right_diag):
    keep = row_mask(rows)
    eye = eye_mask()
    pad = jnp.zeros((8 - TERMS, B), f32)
    lines = []
    for k in range(TERMS):
        block = left[k] * keep
        left2[k] = jnp.concatenate(halves(block), axis=1)
        chosen = jnp.where(shift[k] == 0, 1.0, 0.0).astype(f32)
        lines.append(jnp.sum(jnp.where(eye, block, 0.0), axis=0, keepdims=True) * chosen)
    left_diag[...] = jnp.concatenate(lines + [pad], axis=0)
    lines = [[] for _ in range(LOCAL)]
    for k in range(TERMS):
        for q in range(LOCAL):
            block = right[k, q]
            right2[k, q] = jnp.concatenate(halves(jnp.transpose(block)), axis=1)
            p = group[0] * LOCAL + q
            scale = weights[k * 256 + p * 16 + p]
            lines[q].append(jnp.sum(jnp.where(eye, block, 0.0), axis=0, keepdims=True) * scale)
    for q in range(LOCAL):
        right_diag[q] = jnp.concatenate(lines[q] + [pad], axis=0)
        diag[q] = outer(left_diag[...], right_diag[q])


def mix(group, weights, z, target, outs):
    for half, place in enumerate(outs):
        if place is None:
            continue
        out, at_out = place
        first = target * LOCAL + 2 * half
        acc = [None, None]
        for k in range(TERMS):
            for q in range(LOCAL):
                block = z[k * LOCAL + q]
                for j in range(2):
                    at = k * 256 + (first + j) * 16 + group[0] * LOCAL + q
                    part = weights[at] * block
                    acc[j] = part if acc[j] is None else acc[j] + part
        for j in range(2):
            out[at_out + j] = acc[j]


def terms_kernel(group, sector, shift, weights, own, by_chip, by_core, left2, right2, z, far1, far3, vec2):
    odd = lax.rem(sector[0], 2)
    for p in range(LOCAL):
        vec2[1, p] = jnp.concatenate(halves(own[p]), axis=1)
        vec2[2 - 2 * odd, p] = jnp.concatenate(halves(by_core[p]), axis=1)
        vec2[2 * odd, p] = jnp.concatenate(halves(by_chip[p]), axis=1)
    for k in range(TERMS):
        source = shift[k] + 1
        lhs = left2[k]
        for q in range(LOCAL):
            r = right2[k, q]
            x = jnp.dot(vec2[source, q], jnp.concatenate([r, r], axis=0), preferred_element_type=f32)
            xh, xl = halves(x[:, :B] + x[:, B:])
            both = jnp.concatenate([xh, xl], axis=1)
            y = jnp.dot(lhs, jnp.concatenate([both, both], axis=0), preferred_element_type=f32)
            z[k * LOCAL + q] = y[:, :B] + y[:, B:]
    mix(group, weights, z, group[0] ^ 2, ((far1, 0), (far3, 0)))


def direct_kernel(group, weights, z, direct1, direct3):
    mix(group, weights, z, group[0] ^ 1, ((direct1, 0), None))
    mix(group, weights, z, group[0] ^ 3, (None, (direct3, 0)))


def relayed_kernel(group, weights, z, after, relayed1, relayed3):
    mix(group, weights, z, group[0] ^ 1, (None, (relayed1, 0)))
    mix(group, weights, z, group[0] ^ 3, ((relayed3, 0), None))


def relay_kernel(relayed1, relayed3, got1, got3, out1, out3):
    for j in range(2):
        out1[j] = relayed1[j] + got3[j]
        out3[j] = relayed3[j] + got1[j]


def own_kernel(group, weights, z, own):
    mix(group, weights, z, group[0], ((own, 0), (own, 2)))


def lane(row, j):
    at = lax.broadcasted_iota(jnp.int32, row.shape, 1) == j
    return jnp.sum(jnp.where(at, row, 0.0), axis=1, keepdims=True)


def put_lanes(values):
    at = lax.broadcasted_iota(jnp.int32, (1, B), 1)
    row = jnp.zeros((1, B), f32)
    for j, v in enumerate(values):
        row = jnp.where(at == j, v, row)
    return row


def lowest_root(lead, middle, const):
    root = jnp.sqrt(middle * middle - 4.0 * lead * const)
    return jnp.where(middle > 0, (-middle - root) / (2.0 * lead), 2.0 * const / (root - middle))


def ritz(sums, rayleigh, length):
    s_ic, c_i, curvature, correlation, spread = sums
    cross = 0.5 * (s_ic + c_i)
    lead = length * spread - correlation * correlation
    middle = -(length * curvature + spread * rayleigh - 2.0 * correlation * cross)
    const = rayleigh * curvature - cross * cross
    lowest = lowest_root(lead, middle, const)
    keep = curvature - lowest * spread
    add = lowest * correlation - cross
    norm = keep * keep * length + 2.0 * keep * add * correlation + add * add * spread
    factor = 1.0 / jnp.sqrt(norm)
    keep, add = keep * factor, add * factor
    rayleigh = keep * keep * rayleigh + 2.0 * keep * add * cross + add * add * curvature
    length = keep * keep * length + 2.0 * keep * add * correlation + add * add * spread
    return lowest, keep, add, rayleigh, length


def totals(stats, count, n):
    row = jnp.sum(stats[...], axis=0, keepdims=True) * (1.0 / count)
    return [lane(row, j) for j in range(n)]


def correct(state, image, diag, theta):
    return (image - theta * state) / jnp.maximum(jnp.abs(diag - theta), 1.0)


def start_kernel(count, stats, s0, s1, s2, pack0, pack1, pack2, diag0, right_diag,
                 i0, i1, i2, diag1, diag2, c0, c1, c2, carry):
    rayleigh, length = totals(stats, count, 2)
    theta = rayleigh / length
    for pack, diag in ((pack1, diag1), (pack2, diag2)):
        for p in range(LOCAL):
            diag[p] = outer(pack[LOCAL * B:PACK, :], right_diag[p])
    for s, pack, i, diag, c in ((s0, pack0, i0, diag0, c0), (s1, pack1, i1, diag1, c1), (s2, pack2, i2, diag2, c2)):
        for p in range(LOCAL):
            block = pack[p * B:(p + 1) * B, :]
            i[p] = block
            c[p] = correct(s[p], block, diag[p], theta)
    carry[...] = jnp.broadcast_to(put_lanes([rayleigh, length]), (8, B))


def next_kernel(count, step, keeps, stats, carry_in, *refs):
    sums = totals(stats, count, 5)
    old = carry_in[0:1, :]
    lowest, keep, add, rayleigh, length = ritz(sums, lane(old, 0), lane(old, 1))
    theta = rayleigh / length
    for n in range(3):
        state, image, corr, diag, more = refs[n:15:3]
        for p in range(LOCAL):
            s = keep * state[p] + add * corr[p]
            i = keep * image[p] + add * more[p]
            refs[15 + n][p] = correct(s, i, diag[p], theta)
            if n < keeps:
                refs[18 + n][p] = s
                refs[18 + keeps + n][p] = i
    energies = [lane(old, 2 + j) for j in range(step)] + [lowest]
    refs[-1][...] = jnp.broadcast_to(put_lanes([rayleigh, length] + energies), (8, B))


def last_kernel(count, stats, carry_in, state, corr, state_out, energies):
    sums = totals(stats, count, 5)
    old = carry_in[0:1, :]
    lowest, keep, add, _, _ = ritz(sums, lane(old, 0), lane(old, 1))
    for p in range(LOCAL):
        state_out[p] = keep * state[p] + add * corr[p]
    for j, v in enumerate([lane(old, 2 + j) for j in range(ITERS - 1)] + [lowest]):
        energies[j] = v[0, 0]


def sum_all(block):
    return jnp.sum(jnp.sum(block, axis=0, keepdims=True), axis=1, keepdims=True)


def summed(own, direct1, direct3, relayed1, relayed3, p):
    near, far = (direct1, relayed3) if p < 2 else (relayed1, direct3)
    return own[p] + (near[p % 2] + far[p % 2])


def first_stats_kernel(own, d1, d3, r1, r3, state, left_diag, pack, stats):
    a, b = jnp.zeros((B, B), f32), jnp.zeros((B, B), f32)
    for p in range(LOCAL):
        i = summed(own, d1, d3, r1, r3, p)
        s = state[p]
        pack[p * B:(p + 1) * B, :] = i
        a = a + s * i
        b = b + s * s
    pack[LOCAL * B:PACK, :] = left_diag[...]
    stats[...] = jnp.broadcast_to(put_lanes([sum_all(a), sum_all(b)]), stats.shape)


def stats_kernel(own, d1, d3, r1, r3, state, corr, image, *outs):
    acc = [jnp.zeros((B, B), f32) for _ in range(5)]
    for p in range(LOCAL):
        ic = summed(own, d1, d3, r1, r3, p)
        s, c, i = state[p], corr[p], image[p]
        if len(outs) > 1:
            outs[0][p] = ic
        for j, v in enumerate((s * ic, c * i, c * ic, s * c, c * c)):
            acc[j] = acc[j] + v
    outs[-1][...] = jnp.broadcast_to(put_lanes([sum_all(a) for a in acc]), outs[-1].shape)


def arr(*shape, dtype=f32):
    return jax.ShapeDtypeStruct(shape, dtype)


BLOCK = arr(LOCAL, B, B)
HALF = arr(LOCAL // 2, B, B)
TERM_BLOCKS = arr(TERMS * LOCAL, B, B)


def call(kernel, name, in_specs, outs, scratch=(), out_specs=None, flops=0):
    moved = sum(o.size * o.dtype.itemsize for o in outs)
    return pl.pallas_call(
        kernel,
        out_shape=outs,
        in_specs=in_specs,
        out_specs=out_specs or [VM] * len(outs),
        scratch_shapes=list(scratch),
        compiler_params=PARAMS,
        cost_estimate=pl.CostEstimate(flops=flops, bytes_accessed=2 * moved, transcendentals=0),
        name=name,
    )


def swap(x, step):
    return lax.ppermute(x, "pair", [(i, i ^ step) for i in range(GROUPS)])


def neighbours(x):
    n = lax.axis_size("sec")
    by_chip = lax.ppermute(x, "sec", [(i, i + 1 if i % 2 else i - 1) for i in range(1, n - 1)])
    by_core = lax.ppermute(x, "sec", [(i, i ^ 1) for i in range(n)])
    return by_chip, by_core


def exchange(stats, devices):
    got = lax.all_to_all(stats.reshape(devices, 1, B), ("sec", "pair"), 0, 0)
    return got.reshape(devices, B)


def on_device(psi_start, left_env, right_env, mpo_coef, mpo_pattern, sector_shift, block_rows):
    devices = lax.axis_size("sec") * lax.axis_size("pair")
    count = float(psi_start.size * devices)
    psi = psi_start.reshape(LOCAL, B, B)
    left = left_env.reshape(TERMS, B, B)
    group = lax.axis_index("pair").astype(jnp.int32).reshape(1)
    sector = lax.axis_index("sec").astype(jnp.int32).reshape(1)
    weights = (mpo_coef * mpo_pattern.astype(f32)).reshape(-1)
    stats_shape = arr(devices, B)
    carry_shape = arr(8, B)

    def shares(vectors, left2, right2):
        z, far1, far3 = call(
            terms_kernel, "terms", [SM] * 4 + [VM] * 5, [TERM_BLOCKS, HALF, HALF],
            [pltpu.VMEM((3, LOCAL, B, 2 * B), bf16)],
        )(group, sector, sector_shift, weights, *vectors, left2, right2)
        far1, far3 = swap(far1, 1), swap(far3, 3)
        direct = call(direct_kernel, "direct", [SM, SM, VM], [HALF] * 2)(group, weights, z)
        direct1, direct3 = swap(direct[0], 1), swap(direct[1], 3)
        relayed = call(relayed_kernel, "relayed", [SM, SM, VM, ANY], [HALF] * 2)(group, weights, z, direct[0])
        relayed = call(relay_kernel, "relay", [VM] * 4, [HALF] * 2)(*relayed, far1, far3)
        relayed1, relayed3 = swap(relayed[0], 1), swap(relayed[1], 3)
        (own,) = call(own_kernel, "own", [SM, SM, VM], [BLOCK])(group, weights, z)
        return own, direct1, direct3, relayed1, relayed3

    (state,) = call(mask_kernel, "mask", [SM, VM], [BLOCK])(block_rows, psi)
    states = (state, *neighbours(state))
    left2, right2, diag, left_diag, right_diag = call(
        split_kernel, "split", [SM] * 4 + [VM] * 2,
        [arr(TERMS, B, 2 * B, dtype=bf16), arr(TERMS, LOCAL, B, 2 * B, dtype=bf16), BLOCK, arr(8, B), arr(LOCAL, 8, B)],
    )(group, sector_shift, block_rows, weights, left, right_env)

    parts = shares(states, left2, right2)
    pack, stats = call(first_stats_kernel, "first_stats", [VM] * 7, [arr(PACK, B), stats_shape])(
        *parts, state, left_diag)
    packs = (pack, *neighbours(pack))
    *out, carry = call(
        lambda *refs: start_kernel(count, *refs), "start", [VM] * 9, [BLOCK] * 8 + [carry_shape]
    )(exchange(stats, devices), *states, *packs, diag, right_diag)
    images, diags, corrs = out[:3], (diag, *out[3:5]), out[5:8]

    for step in range(ITERS):
        parts = shares(corrs, left2, right2)
        outs = [BLOCK, stats_shape] if step < ITERS - 1 else [stats_shape]
        *image_corr, stats = call(stats_kernel, "stats", [VM] * 8, outs)(*parts, states[0], corrs[0], images[0])
        got = exchange(stats, devices)
        if step < ITERS - 1:
            more = (*image_corr, *neighbours(*image_corr))
            keeps = 3 if step < ITERS - 2 else 1
            *out, carry = call(
                functools.partial(next_kernel, count, step, keeps), "next", [VM] * 17,
                [BLOCK] * (3 + 2 * keeps) + [carry_shape],
            )(got, carry, *states, *images, *corrs, *diags, *more)
            corrs, states, images = out[:3], out[3:3 + keeps], out[3 + keeps:]

    state, energies = call(
        lambda *refs: last_kernel(count, *refs), "last", [VM] * 4, [BLOCK, arr(ITERS)], out_specs=[VM, SM]
    )(got, carry, states[0], corrs[0])
    return state.reshape(psi_start.shape), energies


def solution(mesh):
    in_specs = (
        P("sec", "pair", None, None),
        P(None, "sec", None, None),
        P(None, "pair", None, None),
        P(),
        P(),
        P(),
        P("sec"),
    )
    out_specs = (P("sec", "pair", None, None), P())
    return jax.shard_map(
        on_device, mesh=mesh, in_specs=in_specs, out_specs=out_specs, check_vma=False
    )
```

```python
import functools

import jax
import jax.numpy as jnp
from jax import lax
from jax.experimental import pallas as pl
from jax.experimental.pallas import tpu as pltpu
from jax.sharding import PartitionSpec as P

ITERS = 4
TERMS = 6
LOCAL = 4
GROUPS = 4
B = 128
PACK = LOCAL * B + 8

f32 = jnp.float32
bf16 = jnp.bfloat16
VM = pl.BlockSpec(memory_space=pltpu.VMEM)
SM = pl.BlockSpec(memory_space=pltpu.SMEM)
ANY = pl.BlockSpec(memory_space=pl.ANY)
PARAMS = pltpu.CompilerParams(vmem_limit_bytes=24 * 1024 * 1024)


def halves(x):
    high = x.astype(bf16)
    return high, (x - high.astype(f32)).astype(bf16)


def eye_mask():
    return lax.broadcasted_iota(jnp.int32, (B, B), 0) == lax.broadcasted_iota(jnp.int32, (B, B), 1)


def row_mask(rows):
    return (lax.broadcasted_iota(jnp.int32, (B, B), 0) < rows[0]).astype(f32)


def mask_kernel(rows, psi, state):
    keep = row_mask(rows)
    for p in range(LOCAL):
        state[p] = psi[p] * keep


def outer(left_lines, right_lines):
    return lax.dot_general(
        left_lines, right_lines, (((0,), (0,)), ((), ())),
        precision=lax.Precision.HIGHEST, preferred_element_type=f32)


def split_kernel(group, shift, rows, weights, left, right, left2, right2, diag, left_diag, right_diag):
    keep = row_mask(rows)
    eye = eye_mask()
    pad = jnp.zeros((8 - TERMS, B), f32)
    lines = []
    for k in range(TERMS):
        block = left[k] * keep
        left2[k] = jnp.concatenate(halves(block), axis=1)
        chosen = jnp.where(shift[k] == 0, 1.0, 0.0).astype(f32)
        lines.append(jnp.sum(jnp.where(eye, block, 0.0), axis=0, keepdims=True) * chosen)
    left_diag[...] = jnp.concatenate(lines + [pad], axis=0)
    lines = [[] for _ in range(LOCAL)]
    for k in range(TERMS):
        for q in range(LOCAL):
            block = right[k, q]
            right2[k, q] = jnp.concatenate(halves(jnp.transpose(block)), axis=1)
            p = group[0] * LOCAL + q
            scale = weights[k * 256 + p * 16 + p]
            lines[q].append(jnp.sum(jnp.where(eye, block, 0.0), axis=0, keepdims=True) * scale)
    for q in range(LOCAL):
        right_diag[q] = jnp.concatenate(lines[q] + [pad], axis=0)
        diag[q] = outer(left_diag[...], right_diag[q])


def mix(group, weights, z, target, out, chunks):
    height = B // chunks

    def part(start, width, at):
        first = target * LOCAL + start
        acc = [None] * width
        for k in range(TERMS):
            for q in range(LOCAL):
                block = z[k * LOCAL + q, at, :]
                for j in range(width):
                    term = weights[k * 256 + (first + j) * 16 + group[0] * LOCAL + q] * block
                    acc[j] = term if acc[j] is None else acc[j] + term
        for j in range(width):
            out[start + j, at, :] = acc[j]

    def rows(r, carry):
        part(0, LOCAL, pl.ds(pl.multiple_of(r * height, height), height))
        return carry

    if chunks > 1:
        lax.fori_loop(0, chunks, rows, 0)
    else:
        for half in range(2):
            part(2 * half, 2, slice(None))


def terms_kernel(group, sector, shift, weights, own, by_chip, by_core, left2, right2, z, far, vec2):
    odd = lax.rem(sector[0], 2)
    for p in range(LOCAL):
        vec2[1, p] = jnp.concatenate(halves(own[p]), axis=1)
        vec2[2 - 2 * odd, p] = jnp.concatenate(halves(by_core[p]), axis=1)
        vec2[2 * odd, p] = jnp.concatenate(halves(by_chip[p]), axis=1)
    for k in range(TERMS):
        source = shift[k] + 1
        lhs = left2[k]
        for q in range(LOCAL):
            r = right2[k, q]
            x = jnp.dot(vec2[source, q], jnp.concatenate([r, r], axis=0), preferred_element_type=f32)
            xh, xl = halves(x[:, :B] + x[:, B:])
            both = jnp.concatenate([xh, xl], axis=1)
            y = jnp.dot(lhs, jnp.concatenate([both, both], axis=0), preferred_element_type=f32)
            z[k * LOCAL + q] = y[:, :B] + y[:, B:]
    mix(group, weights, z, group[0] ^ 2, far, 1)


def direct_kernel(group, sector, weights, z, direct):
    mix(group, weights, z, group[0] ^ (1 + 2 * lax.rem(sector[0], 2)), direct, 2)


def relayed_kernel(group, sector, weights, z, after, relayed):
    mix(group, weights, z, group[0] ^ (3 - 2 * lax.rem(sector[0], 2)), relayed, 4)


def relay_kernel(relayed, far, out):
    for p in range(LOCAL):
        out[p] = relayed[p] + far[p]


def own_kernel(group, weights, z, own):
    mix(group, weights, z, group[0], own, 4)


def lane(row, j):
    at = lax.broadcasted_iota(jnp.int32, row.shape, 1) == j
    return jnp.sum(jnp.where(at, row, 0.0), axis=1, keepdims=True)


def put_lanes(values):
    at = lax.broadcasted_iota(jnp.int32, (1, B), 1)
    row = jnp.zeros((1, B), f32)
    for j, v in enumerate(values):
        row = jnp.where(at == j, v, row)
    return row


def lowest_root(lead, middle, const):
    root = jnp.sqrt(middle * middle - 4.0 * lead * const)
    return jnp.where(middle > 0, (-middle - root) / (2.0 * lead), 2.0 * const / (root - middle))


def ritz(sums, rayleigh, length):
    s_ic, c_i, curvature, correlation, spread = sums
    cross = 0.5 * (s_ic + c_i)
    lead = length * spread - correlation * correlation
    middle = -(length * curvature + spread * rayleigh - 2.0 * correlation * cross)
    const = rayleigh * curvature - cross * cross
    lowest = lowest_root(lead, middle, const)
    keep = curvature - lowest * spread
    add = lowest * correlation - cross
    norm = keep * keep * length + 2.0 * keep * add * correlation + add * add * spread
    factor = 1.0 / jnp.sqrt(norm)
    keep, add = keep * factor, add * factor
    rayleigh = keep * keep * rayleigh + 2.0 * keep * add * cross + add * add * curvature
    length = keep * keep * length + 2.0 * keep * add * correlation + add * add * spread
    return lowest, keep, add, rayleigh, length


def totals(stats, count, n):
    row = jnp.sum(stats[...], axis=0, keepdims=True) * (1.0 / count)
    return [lane(row, j) for j in range(n)]


def correct(state, image, diag, theta):
    return (image - theta * state) / jnp.maximum(jnp.abs(diag - theta), 1.0)


def start_kernel(count, stats, s0, s1, s2, pack0, pack1, pack2, diag0, right_diag,
                 i0, i1, i2, diag1, diag2, c0, c1, c2, carry):
    rayleigh, length = totals(stats, count, 2)
    theta = rayleigh / length
    for pack, diag in ((pack1, diag1), (pack2, diag2)):
        for p in range(LOCAL):
            diag[p] = outer(pack[LOCAL * B:PACK, :], right_diag[p])
    for s, pack, i, diag, c in ((s0, pack0, i0, diag0, c0), (s1, pack1, i1, diag1, c1), (s2, pack2, i2, diag2, c2)):
        for p in range(LOCAL):
            block = pack[p * B:(p + 1) * B, :]
            i[p] = block
            c[p] = correct(s[p], block, diag[p], theta)
    carry[...] = jnp.broadcast_to(put_lanes([rayleigh, length]), (8, B))


def next_kernel(count, step, keeps, stats, carry_in, *refs):
    sums = totals(stats, count, 5)
    old = carry_in[0:1, :]
    lowest, keep, add, rayleigh, length = ritz(sums, lane(old, 0), lane(old, 1))
    theta = rayleigh / length
    for n in range(3):
        state, image, corr, diag, more = refs[n:15:3]
        for p in range(LOCAL):
            s = keep * state[p] + add * corr[p]
            i = keep * image[p] + add * more[p]
            refs[15 + n][p] = correct(s, i, diag[p], theta)
            if n < keeps:
                refs[18 + n][p] = s
                refs[18 + keeps + n][p] = i
    energies = [lane(old, 2 + j) for j in range(step)] + [lowest]
    refs[-1][...] = jnp.broadcast_to(put_lanes([rayleigh, length] + energies), (8, B))


def last_kernel(count, stats, carry_in, state, corr, state_out, energies):
    sums = totals(stats, count, 5)
    old = carry_in[0:1, :]
    lowest, keep, add, _, _ = ritz(sums, lane(old, 0), lane(old, 1))
    for p in range(LOCAL):
        state_out[p] = keep * state[p] + add * corr[p]
    for j, v in enumerate([lane(old, 2 + j) for j in range(ITERS - 1)] + [lowest]):
        energies[j] = v[0, 0]


def sum_all(block):
    return jnp.sum(jnp.sum(block, axis=0, keepdims=True), axis=1, keepdims=True)


def first_stats_kernel(own, direct, relayed, state, left_diag, pack, stats):
    a, b = jnp.zeros((B, B), f32), jnp.zeros((B, B), f32)
    for p in range(LOCAL):
        i = own[p] + (direct[p] + relayed[p])
        s = state[p]
        pack[p * B:(p + 1) * B, :] = i
        a = a + s * i
        b = b + s * s
    pack[LOCAL * B:PACK, :] = left_diag[...]
    stats[...] = jnp.broadcast_to(put_lanes([sum_all(a), sum_all(b)]), stats.shape)


def stats_kernel(own, direct, relayed, state, corr, image, *outs):
    acc = [jnp.zeros((B, B), f32) for _ in range(5)]
    for p in range(LOCAL):
        ic = own[p] + (direct[p] + relayed[p])
        s, c, i = state[p], corr[p], image[p]
        if len(outs) > 1:
            outs[0][p] = ic
        for j, v in enumerate((s * ic, c * i, c * ic, s * c, c * c)):
            acc[j] = acc[j] + v
    outs[-1][...] = jnp.broadcast_to(put_lanes([sum_all(a) for a in acc]), outs[-1].shape)


def arr(*shape, dtype=f32):
    return jax.ShapeDtypeStruct(shape, dtype)


BLOCK = arr(LOCAL, B, B)
TERM_BLOCKS = arr(TERMS * LOCAL, B, B)


def call(kernel, name, in_specs, outs, scratch=(), out_specs=None, flops=0):
    moved = sum(o.size * o.dtype.itemsize for o in outs)
    return pl.pallas_call(
        kernel,
        out_shape=outs,
        in_specs=in_specs,
        out_specs=out_specs or [VM] * len(outs),
        scratch_shapes=list(scratch),
        compiler_params=PARAMS,
        cost_estimate=pl.CostEstimate(flops=flops, bytes_accessed=2 * moved, transcendentals=0),
        name=name,
    )


def swap(x, even, odd):
    n = lax.axis_size("sec")
    perm = [(s * GROUPS + g, s * GROUPS + (g ^ (odd if s % 2 else even))) for s in range(n) for g in range(GROUPS)]
    return lax.ppermute(x, ("sec", "pair"), perm)


def neighbours(x):
    n = lax.axis_size("sec")
    by_chip = lax.ppermute(x, "sec", [(i, i + 1 if i % 2 else i - 1) for i in range(1, n - 1)])
    by_core = lax.ppermute(x, "sec", [(i, i ^ 1) for i in range(n)])
    return by_chip, by_core


def exchange(stats, devices):
    got = lax.all_to_all(stats.reshape(devices, 1, B), ("sec", "pair"), 0, 0)
    return got.reshape(devices, B)


def on_device(psi_start, left_env, right_env, mpo_coef, mpo_pattern, sector_shift, block_rows):
    devices = lax.axis_size("sec") * lax.axis_size("pair")
    count = float(psi_start.size * devices)
    psi = psi_start.reshape(LOCAL, B, B)
    left = left_env.reshape(TERMS, B, B)
    group = lax.axis_index("pair").astype(jnp.int32).reshape(1)
    sector = lax.axis_index("sec").astype(jnp.int32).reshape(1)
    weights = (mpo_coef * mpo_pattern.astype(f32)).reshape(-1)
    stats_shape = arr(devices, B)
    carry_shape = arr(8, B)

    def shares(vectors, left2, right2):
        z, far = call(
            terms_kernel, "terms", [SM] * 4 + [VM] * 5, [TERM_BLOCKS, BLOCK],
            [pltpu.VMEM((3, LOCAL, B, 2 * B), bf16)],
        )(group, sector, sector_shift, weights, *vectors, left2, right2)
        far = swap(far, 1, 3)
        (direct,) = call(direct_kernel, "direct", [SM] * 3 + [VM], [BLOCK])(group, sector, weights, z)
        (relayed,) = call(relayed_kernel, "relayed", [SM] * 3 + [VM, ANY], [BLOCK])(group, sector, weights, z, direct)
        direct = swap(direct, 1, 3)
        (relayed,) = call(relay_kernel, "relay", [VM] * 2, [BLOCK])(relayed, far)
        (own,) = call(own_kernel, "own", [SM, SM, VM], [BLOCK])(group, weights, z)
        return own, direct, swap(relayed, 3, 1)

    (state,) = call(mask_kernel, "mask", [SM, VM], [BLOCK])(block_rows, psi)
    states = (state, *neighbours(state))
    left2, right2, diag, left_diag, right_diag = call(
        split_kernel, "split", [SM] * 4 + [VM] * 2,
        [arr(TERMS, B, 2 * B, dtype=bf16), arr(TERMS, LOCAL, B, 2 * B, dtype=bf16), BLOCK, arr(8, B), arr(LOCAL, 8, B)],
    )(group, sector_shift, block_rows, weights, left, right_env)

    parts = shares(states, left2, right2)
    pack, stats = call(first_stats_kernel, "first_stats", [VM] * 5, [arr(PACK, B), stats_shape])(
        *parts, state, left_diag)
    packs = (pack, *neighbours(pack))
    *out, carry = call(
        lambda *refs: start_kernel(count, *refs), "start", [VM] * 9, [BLOCK] * 8 + [carry_shape]
    )(exchange(stats, devices), *states, *packs, diag, right_diag)
    images, diags, corrs = out[:3], (diag, *out[3:5]), out[5:8]

    for step in range(ITERS):
        parts = shares(corrs, left2, right2)
        outs = [BLOCK, stats_shape] if step < ITERS - 1 else [stats_shape]
        *image_corr, stats = call(stats_kernel, "stats", [VM] * 6, outs)(*parts, states[0], corrs[0], images[0])
        got = exchange(stats, devices)
        if step < ITERS - 1:
            more = (*image_corr, *neighbours(*image_corr))
            keeps = 3 if step < ITERS - 2 else 1
            *out, carry = call(
                functools.partial(next_kernel, count, step, keeps), "next", [VM] * 17,
                [BLOCK] * (3 + 2 * keeps) + [carry_shape],
            )(got, carry, *states, *images, *corrs, *diags, *more)
            corrs, states, images = out[:3], out[3:3 + keeps], out[3 + keeps:]

    state, energies = call(
        lambda *refs: last_kernel(count, *refs), "last", [VM] * 4, [BLOCK, arr(ITERS)], out_specs=[VM, SM]
    )(got, carry, states[0], corrs[0])
    return state.reshape(psi_start.shape), energies


def solution(mesh):
    in_specs = (
        P("sec", "pair", None, None),
        P(None, "sec", None, None),
        P(None, "pair", None, None),
        P(),
        P(),
        P(),
        P("sec"),
    )
    out_specs = (P("sec", "pair", None, None), P())
    return jax.shard_map(
        on_device, mesh=mesh, in_specs=in_specs, out_specs=out_specs, check_vma=False
    )
```

```python
import functools

import jax
import jax.numpy as jnp
from jax import lax
from jax.experimental import pallas as pl
from jax.experimental.pallas import tpu as pltpu
from jax.sharding import PartitionSpec as P

ITERS = 4
TERMS = 6
LOCAL = 4
GROUPS = 4
B = 128
PACK = LOCAL * B + 8

f32 = jnp.float32
bf16 = jnp.bfloat16
VM = pl.BlockSpec(memory_space=pltpu.VMEM)
SM = pl.BlockSpec(memory_space=pltpu.SMEM)
ANY = pl.BlockSpec(memory_space=pl.ANY)
PARAMS = pltpu.CompilerParams(vmem_limit_bytes=24 * 1024 * 1024)


def halves(x):
    high = x.astype(bf16)
    return high, (x - high.astype(f32)).astype(bf16)


def eye_mask():
    return lax.broadcasted_iota(jnp.int32, (B, B), 0) == lax.broadcasted_iota(jnp.int32, (B, B), 1)


def row_mask(rows):
    return (lax.broadcasted_iota(jnp.int32, (B, B), 0) < rows[0]).astype(f32)


def mask_kernel(rows, psi, state):
    keep = row_mask(rows)
    for p in range(LOCAL):
        state[p] = psi[p] * keep


def outer(left_lines, right_lines):
    return lax.dot_general(
        left_lines, right_lines, (((0,), (0,)), ((), ())),
        precision=lax.Precision.HIGHEST, preferred_element_type=f32)


def split_kernel(group, shift, rows, weights, left, right, left2, right2, diag, left_diag, right_diag):
    keep = row_mask(rows)
    eye = eye_mask()
    left_diag[...] = jnp.zeros_like(left_diag)

    def left_term(k, _):
        block = left[k] * keep
        left2[k] = jnp.concatenate(halves(block), axis=1)
        chosen = jnp.where(shift[k] == 0, 1.0, 0.0).astype(f32)
        left_diag[pl.ds(k, 1), :] = jnp.sum(jnp.where(eye, block, 0.0), axis=0, keepdims=True) * chosen
        return 0

    lax.fori_loop(0, TERMS, left_term, 0)
    right_diag[...] = jnp.zeros_like(right_diag)

    def term(k, _):
        for q in range(LOCAL):
            block = right[k, q]
            right2[k, q] = jnp.concatenate(halves(jnp.transpose(block)), axis=1)
            p = group[0] * LOCAL + q
            scale = weights[k * 256 + p * 16 + p]
            right_diag[q, pl.ds(k, 1), :] = jnp.sum(jnp.where(eye, block, 0.0), axis=0, keepdims=True) * scale
        return 0

    lax.fori_loop(0, TERMS, term, 0)

    def outer_block(q, _):
        diag[q] = outer(left_diag[...], right_diag[q])
        return 0

    lax.fori_loop(0, LOCAL, outer_block, 0)


def mix(group, weights, z, target, out, chunks):
    height = B // chunks

    def part(start, width, at, out, place):
        first = target * LOCAL + start
        acc = [None] * width
        for k in range(TERMS):
            for q in range(LOCAL):
                block = z[k * LOCAL + q, at, :]
                for j in range(width):
                    term = weights[k * 256 + (first + j) * 16 + group[0] * LOCAL + q] * block
                    acc[j] = term if acc[j] is None else acc[j] + term
        for j in range(width):
            out[place + j, at, :] = acc[j]

    def rows(r, carry):
        part(0, LOCAL, pl.ds(pl.multiple_of(r * height, height), height), out, 0)
        return carry

    if chunks > 1:
        lax.fori_loop(0, chunks, rows, 0)
    else:
        for half in range(2):
            part(2 * half, 2, slice(None), out[half], 0)


def terms_kernel(group, sector, shift, weights, own, by_chip, by_core, left2, right2, z, far_a, far_b, vec2):
    odd = lax.rem(sector[0], 2)
    for p in range(LOCAL):
        vec2[1, p] = jnp.concatenate(halves(own[p]), axis=1)
        vec2[2 - 2 * odd, p] = jnp.concatenate(halves(by_core[p]), axis=1)
        vec2[2 * odd, p] = jnp.concatenate(halves(by_chip[p]), axis=1)
    for k in range(TERMS):
        source = shift[k] + 1
        lhs = left2[k]
        for q in range(LOCAL):
            r = right2[k, q]
            x = jnp.dot(vec2[source, q], jnp.concatenate([r, r], axis=0), preferred_element_type=f32)
            xh, xl = halves(x[:, :B] + x[:, B:])
            both = jnp.concatenate([xh, xl], axis=1)
            y = jnp.dot(lhs, jnp.concatenate([both, both], axis=0), preferred_element_type=f32)
            z[k * LOCAL + q] = y[:, :B] + y[:, B:]
    mix(group, weights, z, group[0] ^ 2, (far_a, far_b), 1)


def direct_kernel(group, sector, weights, z, direct):
    mix(group, weights, z, group[0] ^ (1 + 2 * lax.rem(sector[0], 2)), direct, 4)


def relayed_kernel(group, sector, weights, z, after, relayed):
    mix(group, weights, z, group[0] ^ (3 - 2 * lax.rem(sector[0], 2)), relayed, 4)


def relay_kernel(relayed, far_a, far_b, out_a, out_b):
    for j in range(2):
        out_a[j] = relayed[j] + far_a[j]
        out_b[j] = relayed[2 + j] + far_b[j]


def own_kernel(group, weights, z, own):
    mix(group, weights, z, group[0], own, 4)


def lane(row, j):
    at = lax.broadcasted_iota(jnp.int32, row.shape, 1) == j
    return jnp.sum(jnp.where(at, row, 0.0), axis=1, keepdims=True)


def put_lanes(values):
    at = lax.broadcasted_iota(jnp.int32, (1, B), 1)
    row = jnp.zeros((1, B), f32)
    for j, v in enumerate(values):
        row = jnp.where(at == j, v, row)
    return row


def lowest_root(lead, middle, const):
    root = jnp.sqrt(middle * middle - 4.0 * lead * const)
    return jnp.where(middle > 0, (-middle - root) / (2.0 * lead), 2.0 * const / (root - middle))


def ritz(sums, rayleigh, length):
    s_ic, c_i, curvature, correlation, spread = sums
    cross = 0.5 * (s_ic + c_i)
    lead = length * spread - correlation * correlation
    middle = -(length * curvature + spread * rayleigh - 2.0 * correlation * cross)
    const = rayleigh * curvature - cross * cross
    lowest = lowest_root(lead, middle, const)
    keep = curvature - lowest * spread
    add = lowest * correlation - cross
    norm = keep * keep * length + 2.0 * keep * add * correlation + add * add * spread
    factor = 1.0 / jnp.sqrt(norm)
    keep, add = keep * factor, add * factor
    rayleigh = keep * keep * rayleigh + 2.0 * keep * add * cross + add * add * curvature
    length = keep * keep * length + 2.0 * keep * add * correlation + add * add * spread
    return lowest, keep, add, rayleigh, length


def totals(stats, count, n):
    row = jnp.sum(stats[...], axis=0, keepdims=True) * (1.0 / count)
    return [lane(row, j) for j in range(n)]


def correct(state, image, diag, theta):
    return (image - theta * state) / jnp.maximum(jnp.abs(diag - theta), 1.0)


def start_kernel(count, stats, s0, s1, s2, pack0, pack1, pack2, diag0, right_diag,
                 i0, i1, i2, diag1, diag2, c0, c1, c2, carry):
    rayleigh, length = totals(stats, count, 2)
    theta = rayleigh / length
    blocks = ((s0, pack0, i0, diag0, c0), (s1, pack1, i1, diag1, c1), (s2, pack2, i2, diag2, c2))

    def block(p, _):
        for n, (s, pack, i, diag, c) in enumerate(blocks):
            if n:
                diag[p] = outer(pack[LOCAL * B:PACK, :], right_diag[p])
            image = pack[pl.ds(pl.multiple_of(p * B, B), B), :]
            i[p] = image
            c[p] = correct(s[p], image, diag[p], theta)
        return 0

    lax.fori_loop(0, LOCAL, block, 0)
    carry[...] = jnp.broadcast_to(put_lanes([rayleigh, length]), (8, B))


def next_kernel(count, step, keeps, stats, carry_in, *refs):
    sums = totals(stats, count, 5)
    old = carry_in[0:1, :]
    lowest, keep, add, rayleigh, length = ritz(sums, lane(old, 0), lane(old, 1))
    theta = rayleigh / length
    for n in range(3):
        state, image, corr, diag, more = refs[n:15:3]
        def body(p, _):
            s = keep * state[p] + add * corr[p]
            i = keep * image[p] + add * more[p]
            refs[15 + n][p] = correct(s, i, diag[p], theta)
            if n < keeps:
                refs[18 + n][p] = s
                refs[18 + keeps + n][p] = i
            return 0

        lax.fori_loop(0, LOCAL, body, 0)
    energies = [lane(old, 2 + j) for j in range(step)] + [lowest]
    refs[-1][...] = jnp.broadcast_to(put_lanes([rayleigh, length] + energies), (8, B))


def last_kernel(count, stats, carry_in, state, corr, state_out, energies):
    sums = totals(stats, count, 5)
    old = carry_in[0:1, :]
    lowest, keep, add, _, _ = ritz(sums, lane(old, 0), lane(old, 1))
    for p in range(LOCAL):
        state_out[p] = keep * state[p] + add * corr[p]
    for j, v in enumerate([lane(old, 2 + j) for j in range(ITERS - 1)] + [lowest]):
        energies[j] = v[0, 0]


def sum_all(block):
    return jnp.sum(jnp.sum(block, axis=0, keepdims=True), axis=1, keepdims=True)


def first_stats_kernel(own, direct, relayed_a, relayed_b, state, left_diag, pack, stats):
    a, b = jnp.zeros((B, B), f32), jnp.zeros((B, B), f32)
    for p in range(LOCAL):
        i = own[p] + (direct[p] + (relayed_a, relayed_b)[p // 2][p % 2])
        s = state[p]
        pack[p * B:(p + 1) * B, :] = i
        a = a + s * i
        b = b + s * s
    pack[LOCAL * B:PACK, :] = left_diag[...]
    stats[...] = jnp.broadcast_to(put_lanes([sum_all(a), sum_all(b)]), stats.shape)


def stats_kernel(own, direct, relayed_a, relayed_b, state, corr, image, *outs):
    acc = [jnp.zeros((B, B), f32) for _ in range(5)]
    for p in range(LOCAL):
        ic = own[p] + (direct[p] + (relayed_a, relayed_b)[p // 2][p % 2])
        s, c, i = state[p], corr[p], image[p]
        if len(outs) > 1:
            outs[0][p] = ic
        for j, v in enumerate((s * ic, c * i, c * ic, s * c, c * c)):
            acc[j] = acc[j] + v
    outs[-1][...] = jnp.broadcast_to(put_lanes([sum_all(a) for a in acc]), outs[-1].shape)


def arr(*shape, dtype=f32):
    return jax.ShapeDtypeStruct(shape, dtype)


BLOCK = arr(LOCAL, B, B)
HALF = arr(LOCAL // 2, B, B)
TERM_BLOCKS = arr(TERMS * LOCAL, B, B)


def call(kernel, name, in_specs, outs, scratch=(), out_specs=None, flops=0):
    moved = sum(o.size * o.dtype.itemsize for o in outs)
    return pl.pallas_call(
        kernel,
        out_shape=outs,
        in_specs=in_specs,
        out_specs=out_specs or [VM] * len(outs),
        scratch_shapes=list(scratch),
        compiler_params=PARAMS,
        cost_estimate=pl.CostEstimate(flops=flops, bytes_accessed=2 * moved, transcendentals=0),
        name=name,
    )


def swap(x, even, odd):
    n = lax.axis_size("sec")
    perm = [(s * GROUPS + g, s * GROUPS + (g ^ (odd if s % 2 else even))) for s in range(n) for g in range(GROUPS)]
    return lax.ppermute(x, ("sec", "pair"), perm)


def neighbours(x):
    n = lax.axis_size("sec")
    by_chip = lax.ppermute(x, "sec", [(i, i + 1 if i % 2 else i - 1) for i in range(1, n - 1)])
    by_core = lax.ppermute(x, "sec", [(i, i ^ 1) for i in range(n)])
    return by_chip, by_core


def exchange(stats, devices):
    got = lax.all_to_all(stats.reshape(devices, 1, B), ("sec", "pair"), 0, 0)
    return got.reshape(devices, B)


def on_device(psi_start, left_env, right_env, mpo_coef, mpo_pattern, sector_shift, block_rows):
    devices = lax.axis_size("sec") * lax.axis_size("pair")
    count = float(psi_start.size * devices)
    psi = psi_start.reshape(LOCAL, B, B)
    left = left_env.reshape(TERMS, B, B)
    group = lax.axis_index("pair").astype(jnp.int32).reshape(1)
    sector = lax.axis_index("sec").astype(jnp.int32).reshape(1)
    weights = (mpo_coef * mpo_pattern.astype(f32)).reshape(-1)
    stats_shape = arr(devices, B)
    carry_shape = arr(8, B)

    def shares(vectors, left2, right2):
        z, *far = call(
            terms_kernel, "terms", [SM] * 4 + [VM] * 5, [TERM_BLOCKS, HALF, HALF],
            [pltpu.VMEM((3, LOCAL, B, 2 * B), bf16)],
        )(group, sector, sector_shift, weights, *vectors, left2, right2)
        far = [swap(x, 1, 3) for x in far]
        (direct,) = call(direct_kernel, "direct", [SM] * 3 + [VM], [BLOCK])(group, sector, weights, z)
        (relayed,) = call(relayed_kernel, "relayed", [SM] * 3 + [VM, ANY], [BLOCK])(group, sector, weights, z, direct)
        direct = swap(direct, 1, 3)
        relayed = call(relay_kernel, "relay", [VM] * 3, [HALF] * 2)(relayed, *far)
        (own,) = call(own_kernel, "own", [SM, SM, VM], [BLOCK])(group, weights, z)
        return own, direct, *(swap(x, 3, 1) for x in relayed)

    (state,) = call(mask_kernel, "mask", [SM, VM], [BLOCK])(block_rows, psi)
    states = (state, *neighbours(state))
    left2, right2, diag, left_diag, right_diag = call(
        split_kernel, "split", [SM] * 4 + [VM] * 2,
        [arr(TERMS, B, 2 * B, dtype=bf16), arr(TERMS, LOCAL, B, 2 * B, dtype=bf16), BLOCK, arr(8, B), arr(LOCAL, 8, B)],
    )(group, sector_shift, block_rows, weights, left, right_env)

    parts = shares(states, left2, right2)
    pack, stats = call(first_stats_kernel, "first_stats", [VM] * 6, [arr(PACK, B), stats_shape])(
        *parts, state, left_diag)
    packs = (pack, *neighbours(pack))
    *out, carry = call(
        lambda *refs: start_kernel(count, *refs), "start", [VM] * 9, [BLOCK] * 8 + [carry_shape]
    )(exchange(stats, devices), *states, *packs, diag, right_diag)
    images, diags, corrs = out[:3], (diag, *out[3:5]), out[5:8]

    for step in range(ITERS):
        parts = shares(corrs, left2, right2)
        outs = [BLOCK, stats_shape] if step < ITERS - 1 else [stats_shape]
        *image_corr, stats = call(stats_kernel, "stats", [VM] * 7, outs)(*parts, states[0], corrs[0], images[0])
        got = exchange(stats, devices)
        if step < ITERS - 1:
            more = (*image_corr, *neighbours(*image_corr))
            keeps = 3 if step < ITERS - 2 else 1
            *out, carry = call(
                functools.partial(next_kernel, count, step, keeps), "next", [VM] * 17,
                [BLOCK] * (3 + 2 * keeps) + [carry_shape],
            )(got, carry, *states, *images, *corrs, *diags, *more)
            corrs, states, images = out[:3], out[3:3 + keeps], out[3 + keeps:]

    state, energies = call(
        lambda *refs: last_kernel(count, *refs), "last", [VM] * 4, [BLOCK, arr(ITERS)], out_specs=[VM, SM]
    )(got, carry, states[0], corrs[0])
    return state.reshape(psi_start.shape), energies


def solution(mesh):
    in_specs = (
        P("sec", "pair", None, None),
        P(None, "sec", None, None),
        P(None, "pair", None, None),
        P(),
        P(),
        P(),
        P("sec"),
    )
    out_specs = (P("sec", "pair", None, None), P())
    return jax.shard_map(
        on_device, mesh=mesh, in_specs=in_specs, out_specs=out_specs, check_vma=False
    )
```

```python
import functools

import jax
import jax.numpy as jnp
from jax import lax
from jax.experimental import pallas as pl
from jax.experimental.pallas import tpu as pltpu
from jax.sharding import PartitionSpec as P

ITERS = 4
TERMS = 6
LOCAL = 4
GROUPS = 4
B = 128
PACK = LOCAL * B + 8

f32 = jnp.float32
bf16 = jnp.bfloat16
VM = pl.BlockSpec(memory_space=pltpu.VMEM)
SM = pl.BlockSpec(memory_space=pltpu.SMEM)
ANY = pl.BlockSpec(memory_space=pl.ANY)
PARAMS = pltpu.CompilerParams(vmem_limit_bytes=24 * 1024 * 1024)


def halves(x):
    high = x.astype(bf16)
    return high, (x - high.astype(f32)).astype(bf16)


def eye_mask():
    return lax.broadcasted_iota(jnp.int32, (B, B), 0) == lax.broadcasted_iota(jnp.int32, (B, B), 1)


def row_mask(rows):
    return (lax.broadcasted_iota(jnp.int32, (B, B), 0) < rows[0]).astype(f32)


def mask_kernel(rows, psi, state):
    keep = row_mask(rows)
    for p in range(LOCAL):
        state[p] = psi[p] * keep


def outer(left_lines, right_lines):
    return lax.dot_general(
        left_lines, right_lines, (((0,), (0,)), ((), ())),
        precision=lax.Precision.HIGHEST, preferred_element_type=f32)


def split_kernel(group, shift, rows, weights, left, right, left2, right2, diag, left_diag, right_diag):
    keep = row_mask(rows)
    eye = eye_mask()
    pad = jnp.zeros((8 - TERMS, B), f32)
    lines = []
    for k in range(TERMS):
        block = left[k] * keep
        left2[k] = jnp.concatenate(halves(block), axis=1)
        chosen = jnp.where(shift[k] == 0, 1.0, 0.0).astype(f32)
        lines.append(jnp.sum(jnp.where(eye, block, 0.0), axis=0, keepdims=True) * chosen)
    left_diag[...] = jnp.concatenate(lines + [pad], axis=0)
    lines = [[] for _ in range(LOCAL)]
    for k in range(TERMS):
        for q in range(LOCAL):
            block = right[k, q]
            right2[k, q] = jnp.concatenate(halves(jnp.transpose(block)), axis=1)
            p = group[0] * LOCAL + q
            scale = weights[k * 256 + p * 16 + p]
            lines[q].append(jnp.sum(jnp.where(eye, block, 0.0), axis=0, keepdims=True) * scale)
    for q in range(LOCAL):
        right_diag[q] = jnp.concatenate(lines[q] + [pad], axis=0)
        diag[q] = outer(left_diag[...], right_diag[q])


def mix(group, weights, z, target, out, chunks):
    height = B // chunks

    def part(start, width, at, out, place):
        first = target * LOCAL + start
        acc = [None] * width
        for k in range(TERMS):
            for q in range(LOCAL):
                block = z[k * LOCAL + q, at, :]
                for j in range(width):
                    term = weights[k * 256 + (first + j) * 16 + group[0] * LOCAL + q] * block
                    acc[j] = term if acc[j] is None else acc[j] + term
        for j in range(width):
            out[place + j, at, :] = acc[j]

    def rows(r, carry):
        part(0, LOCAL, pl.ds(pl.multiple_of(r * height, height), height), out, 0)
        return carry

    if chunks > 1:
        lax.fori_loop(0, chunks, rows, 0)
    else:
        for half in range(2):
            if isinstance(out, tuple):
                part(2 * half, 2, slice(None), out[half], 0)
            else:
                part(2 * half, 2, slice(None), out, 2 * half)


def terms_kernel(group, sector, shift, weights, own, by_chip, by_core, left2, right2, z, *refs):
    *far, vec2 = refs
    odd = lax.rem(sector[0], 2)
    for p in range(LOCAL):
        vec2[1, p] = jnp.concatenate(halves(own[p]), axis=1)
        vec2[2 - 2 * odd, p] = jnp.concatenate(halves(by_core[p]), axis=1)
        vec2[2 * odd, p] = jnp.concatenate(halves(by_chip[p]), axis=1)
    for k in range(TERMS):
        source = shift[k] + 1
        lhs = left2[k]
        for q in range(LOCAL):
            r = right2[k, q]
            x = jnp.dot(vec2[source, q], jnp.concatenate([r, r], axis=0), preferred_element_type=f32)
            xh, xl = halves(x[:, :B] + x[:, B:])
            both = jnp.concatenate([xh, xl], axis=1)
            y = jnp.dot(lhs, jnp.concatenate([both, both], axis=0), preferred_element_type=f32)
            z[k * LOCAL + q] = y[:, :B] + y[:, B:]
    mix(group, weights, z, group[0] ^ 2, tuple(far) if len(far) > 1 else far[0], 1)


def direct_kernel(group, sector, weights, z, direct):
    mix(group, weights, z, group[0] ^ (1 + 2 * lax.rem(sector[0], 2)), direct, 2)


def relayed_kernel(group, sector, weights, z, after, relayed):
    mix(group, weights, z, group[0] ^ (3 - 2 * lax.rem(sector[0], 2)), relayed, 4)


def relay_kernel(first, relayed, far, out):
    for p in range(far.shape[0]):
        out[p] = relayed[first + p] + far[p]


def own_kernel(group, weights, z, own):
    mix(group, weights, z, group[0], own, 4)


def lane(row, j):
    at = lax.broadcasted_iota(jnp.int32, row.shape, 1) == j
    return jnp.sum(jnp.where(at, row, 0.0), axis=1, keepdims=True)


def put_lanes(values):
    at = lax.broadcasted_iota(jnp.int32, (1, B), 1)
    row = jnp.zeros((1, B), f32)
    for j, v in enumerate(values):
        row = jnp.where(at == j, v, row)
    return row


def lowest_root(lead, middle, const):
    root = jnp.sqrt(middle * middle - 4.0 * lead * const)
    return jnp.where(middle > 0, (-middle - root) / (2.0 * lead), 2.0 * const / (root - middle))


def ritz(sums, rayleigh, length):
    s_ic, c_i, curvature, correlation, spread = sums
    cross = 0.5 * (s_ic + c_i)
    lead = length * spread - correlation * correlation
    middle = -(length * curvature + spread * rayleigh - 2.0 * correlation * cross)
    const = rayleigh * curvature - cross * cross
    lowest = lowest_root(lead, middle, const)
    keep = curvature - lowest * spread
    add = lowest * correlation - cross
    norm = keep * keep * length + 2.0 * keep * add * correlation + add * add * spread
    factor = 1.0 / jnp.sqrt(norm)
    keep, add = keep * factor, add * factor
    rayleigh = keep * keep * rayleigh + 2.0 * keep * add * cross + add * add * curvature
    length = keep * keep * length + 2.0 * keep * add * correlation + add * add * spread
    return lowest, keep, add, rayleigh, length


def totals(stats, count, n):
    row = jnp.sum(stats[...], axis=0, keepdims=True) * (1.0 / count)
    return [lane(row, j) for j in range(n)]


def correct(state, image, diag, theta):
    return (image - theta * state) / jnp.maximum(jnp.abs(diag - theta), 1.0)


def start_kernel(count, stats, s0, s1, s2, pack0, pack1, pack2, diag0, right_diag,
                 i0, i1, i2, diag1, diag2, c0, c1, c2, carry):
    rayleigh, length = totals(stats, count, 2)
    theta = rayleigh / length
    for pack, diag in ((pack1, diag1), (pack2, diag2)):
        for p in range(LOCAL):
            diag[p] = outer(pack[LOCAL * B:PACK, :], right_diag[p])
    for s, pack, i, diag, c in ((s0, pack0, i0, diag0, c0), (s1, pack1, i1, diag1, c1), (s2, pack2, i2, diag2, c2)):
        for p in range(LOCAL):
            block = pack[p * B:(p + 1) * B, :]
            i[p] = block
            c[p] = correct(s[p], block, diag[p], theta)
    carry[...] = jnp.broadcast_to(put_lanes([rayleigh, length]), (8, B))


def next_kernel(count, step, keeps, stats, carry_in, *refs):
    sums = totals(stats, count, 5)
    old = carry_in[0:1, :]
    lowest, keep, add, rayleigh, length = ritz(sums, lane(old, 0), lane(old, 1))
    theta = rayleigh / length
    for n in range(3):
        state, image, corr, diag, more = refs[n:15:3]
        for p in range(LOCAL):
            s = keep * state[p] + add * corr[p]
            i = keep * image[p] + add * more[p]
            refs[15 + n][p] = correct(s, i, diag[p], theta)
            if n < keeps:
                refs[18 + n][p] = s
                refs[18 + keeps + n][p] = i
    energies = [lane(old, 2 + j) for j in range(step)] + [lowest]
    refs[-1][...] = jnp.broadcast_to(put_lanes([rayleigh, length] + energies), (8, B))


def last_kernel(count, stats, carry_in, state, corr, state_out, energies):
    sums = totals(stats, count, 5)
    old = carry_in[0:1, :]
    lowest, keep, add, _, _ = ritz(sums, lane(old, 0), lane(old, 1))
    for p in range(LOCAL):
        state_out[p] = keep * state[p] + add * corr[p]
    for j, v in enumerate([lane(old, 2 + j) for j in range(ITERS - 1)] + [lowest]):
        energies[j] = v[0, 0]


def sum_all(block):
    return jnp.sum(jnp.sum(block, axis=0, keepdims=True), axis=1, keepdims=True)


def summed(own, direct, relayed, p):
    width = LOCAL // len(relayed)
    return own[p] + (direct[p] + relayed[p // width][p % width])


def first_stats_kernel(own, direct, relayed, state, left_diag, pack, stats):
    a, b = jnp.zeros((B, B), f32), jnp.zeros((B, B), f32)
    for p in range(LOCAL):
        i = summed(own, direct, (relayed,), p)
        s = state[p]
        pack[p * B:(p + 1) * B, :] = i
        a = a + s * i
        b = b + s * s
    pack[LOCAL * B:PACK, :] = left_diag[...]
    stats[...] = jnp.broadcast_to(put_lanes([sum_all(a), sum_all(b)]), stats.shape)


def stats_kernel(streams, own, direct, *refs):
    relayed, (state, corr, image), outs = refs[:streams], refs[streams:streams + 3], refs[streams + 3:]
    acc = [jnp.zeros((B, B), f32) for _ in range(5)]
    for p in range(LOCAL):
        ic = summed(own, direct, relayed, p)
        s, c, i = state[p], corr[p], image[p]
        if len(outs) > 1:
            outs[0][p] = ic
        for j, v in enumerate((s * ic, c * i, c * ic, s * c, c * c)):
            acc[j] = acc[j] + v
    outs[-1][...] = jnp.broadcast_to(put_lanes([sum_all(a) for a in acc]), outs[-1].shape)


def arr(*shape, dtype=f32):
    return jax.ShapeDtypeStruct(shape, dtype)


BLOCK = arr(LOCAL, B, B)
TERM_BLOCKS = arr(TERMS * LOCAL, B, B)


def call(kernel, name, in_specs, outs, scratch=(), out_specs=None, flops=0):
    moved = sum(o.size * o.dtype.itemsize for o in outs)
    return pl.pallas_call(
        kernel,
        out_shape=outs,
        in_specs=in_specs,
        out_specs=out_specs or [VM] * len(outs),
        scratch_shapes=list(scratch),
        compiler_params=PARAMS,
        cost_estimate=pl.CostEstimate(flops=flops, bytes_accessed=2 * moved, transcendentals=0),
        name=name,
    )


def swap(x, even, odd):
    n = lax.axis_size("sec")
    perm = [(s * GROUPS + g, s * GROUPS + (g ^ (odd if s % 2 else even))) for s in range(n) for g in range(GROUPS)]
    return lax.ppermute(x, ("sec", "pair"), perm)


def neighbours(x):
    n = lax.axis_size("sec")
    by_chip = lax.ppermute(x, "sec", [(i, i + 1 if i % 2 else i - 1) for i in range(1, n - 1)])
    by_core = lax.ppermute(x, "sec", [(i, i ^ 1) for i in range(n)])
    return by_chip, by_core


def exchange(stats, devices):
    got = lax.all_to_all(stats.reshape(devices, 1, B), ("sec", "pair"), 0, 0)
    return got.reshape(devices, B)


def on_device(psi_start, left_env, right_env, mpo_coef, mpo_pattern, sector_shift, block_rows):
    devices = lax.axis_size("sec") * lax.axis_size("pair")
    count = float(psi_start.size * devices)
    psi = psi_start.reshape(LOCAL, B, B)
    left = left_env.reshape(TERMS, B, B)
    group = lax.axis_index("pair").astype(jnp.int32).reshape(1)
    sector = lax.axis_index("sec").astype(jnp.int32).reshape(1)
    weights = (mpo_coef * mpo_pattern.astype(f32)).reshape(-1)
    stats_shape = arr(devices, B)
    carry_shape = arr(8, B)

    def shares(vectors, left2, right2, streams):
        width = LOCAL // streams
        z, *far = call(
            terms_kernel, "terms", [SM] * 4 + [VM] * 5, [TERM_BLOCKS] + [arr(width, B, B)] * streams,
            [pltpu.VMEM((3, LOCAL, B, 2 * B), bf16)],
        )(group, sector, sector_shift, weights, *vectors, left2, right2)
        far = [swap(x, 1, 3) for x in far]
        (direct,) = call(direct_kernel, "direct", [SM] * 3 + [VM], [BLOCK])(group, sector, weights, z)
        (relayed,) = call(relayed_kernel, "relayed", [SM] * 3 + [VM, ANY], [BLOCK])(group, sector, weights, z, direct)
        direct = swap(direct, 1, 3)
        relayed = [
            swap(call(functools.partial(relay_kernel, n * width), "relay", [VM] * 2, [arr(width, B, B)])(relayed, x)[0], 3, 1)
            for n, x in enumerate(far)
        ]
        (own,) = call(own_kernel, "own", [SM, SM, VM], [BLOCK])(group, weights, z)
        return own, direct, *relayed

    (state,) = call(mask_kernel, "mask", [SM, VM], [BLOCK])(block_rows, psi)
    states = (state, *neighbours(state))
    left2, right2, diag, left_diag, right_diag = call(
        split_kernel, "split", [SM] * 4 + [VM] * 2,
        [arr(TERMS, B, 2 * B, dtype=bf16), arr(TERMS, LOCAL, B, 2 * B, dtype=bf16), BLOCK, arr(8, B), arr(LOCAL, 8, B)],
    )(group, sector_shift, block_rows, weights, left, right_env)

    parts = shares(states, left2, right2, 1)
    pack, stats = call(first_stats_kernel, "first_stats", [VM] * 5, [arr(PACK, B), stats_shape])(
        *parts, state, left_diag)
    packs = (pack, *neighbours(pack))
    *out, carry = call(
        lambda *refs: start_kernel(count, *refs), "start", [VM] * 9, [BLOCK] * 8 + [carry_shape]
    )(exchange(stats, devices), *states, *packs, diag, right_diag)
    images, diags, corrs = out[:3], (diag, *out[3:5]), out[5:8]

    for step in range(ITERS):
        streams = 2 if step < ITERS - 1 else 1
        parts = shares(corrs, left2, right2, streams)
        outs = [BLOCK, stats_shape] if step < ITERS - 1 else [stats_shape]
        *image_corr, stats = call(functools.partial(stats_kernel, streams), "stats", [VM] * (5 + streams), outs)(
            *parts, states[0], corrs[0], images[0])
        got = exchange(stats, devices)
        if step < ITERS - 1:
            more = (*image_corr, *neighbours(*image_corr))
            keeps = 3 if step < ITERS - 2 else 1
            *out, carry = call(
                functools.partial(next_kernel, count, step, keeps), "next", [VM] * 17,
                [BLOCK] * (3 + 2 * keeps) + [carry_shape],
            )(got, carry, *states, *images, *corrs, *diags, *more)
            corrs, states, images = out[:3], out[3:3 + keeps], out[3 + keeps:]

    state, energies = call(
        lambda *refs: last_kernel(count, *refs), "last", [VM] * 4, [BLOCK, arr(ITERS)], out_specs=[VM, SM]
    )(got, carry, states[0], corrs[0])
    return state.reshape(psi_start.shape), energies


def solution(mesh):
    in_specs = (
        P("sec", "pair", None, None),
        P(None, "sec", None, None),
        P(None, "pair", None, None),
        P(),
        P(),
        P(),
        P("sec"),
    )
    out_specs = (P("sec", "pair", None, None), P())
    return jax.shard_map(
        on_device, mesh=mesh, in_specs=in_specs, out_specs=out_specs, check_vma=False
    )
```

```python
import functools

import jax
import jax.numpy as jnp
from jax import lax
from jax.experimental import pallas as pl
from jax.experimental.pallas import tpu as pltpu
from jax.sharding import PartitionSpec as P

ITERS = 4
TERMS = 6
LOCAL = 4
GROUPS = 4
B = 128
PACK = LOCAL * B + 16
THETA = 16

f32 = jnp.float32
bf16 = jnp.bfloat16
VM = pl.BlockSpec(memory_space=pltpu.VMEM)
SM = pl.BlockSpec(memory_space=pltpu.SMEM)
ANY = pl.BlockSpec(memory_space=pl.ANY)
PARAMS = pltpu.CompilerParams(vmem_limit_bytes=24 * 1024 * 1024)


def halves(x):
    high = x.astype(bf16)
    return high, (x - high.astype(f32)).astype(bf16)


def eye_mask():
    return lax.broadcasted_iota(jnp.int32, (B, B), 0) == lax.broadcasted_iota(jnp.int32, (B, B), 1)


def row_mask(rows):
    return (lax.broadcasted_iota(jnp.int32, (B, B), 0) < rows[0]).astype(f32)


def mask_kernel(rows, psi, state):
    keep = row_mask(rows)
    for p in range(LOCAL):
        state[p] = psi[p] * keep


def outer(left_lines, right_lines):
    return lax.dot_general(
        left_lines, right_lines, (((0,), (0,)), ((), ())),
        precision=lax.Precision.HIGHEST, preferred_element_type=f32)


def split_kernel(group, shift, rows, weights, left, right, left2, right2, diag, left_diag, right_diag):
    keep = row_mask(rows)
    eye = eye_mask()
    pad = jnp.zeros((8 - TERMS, B), f32)
    lines = []
    for k in range(TERMS):
        block = left[k] * keep
        left2[k] = jnp.concatenate(halves(block), axis=1)
        chosen = jnp.where(shift[k] == 0, 1.0, 0.0).astype(f32)
        lines.append(jnp.sum(jnp.where(eye, block, 0.0), axis=0, keepdims=True) * chosen)
    left_diag[...] = jnp.concatenate(lines + [pad], axis=0)
    lines = [[] for _ in range(LOCAL)]
    for k in range(TERMS):
        for q in range(LOCAL):
            block = right[k, q]
            right2[k, q] = jnp.concatenate(halves(jnp.transpose(block)), axis=1)
            p = group[0] * LOCAL + q
            scale = weights[k * 256 + p * 16 + p]
            lines[q].append(jnp.sum(jnp.where(eye, block, 0.0), axis=0, keepdims=True) * scale)
    for q in range(LOCAL):
        right_diag[q] = jnp.concatenate(lines[q] + [pad], axis=0)
        diag[q] = outer(left_diag[...], right_diag[q])


def mix(group, weights, z, target, out, chunks):
    height = B // chunks

    def part(start, width, at):
        first = target * LOCAL + start
        acc = [None] * width
        for k in range(TERMS):
            for q in range(LOCAL):
                block = z[k * LOCAL + q, at, :]
                for j in range(width):
                    term = weights[k * 256 + (first + j) * 16 + group[0] * LOCAL + q] * block
                    acc[j] = term if acc[j] is None else acc[j] + term
        for j in range(width):
            out[start + j, at, :] = acc[j]

    def rows(r, carry):
        part(0, LOCAL, pl.ds(pl.multiple_of(r * height, height), height))
        return carry

    if chunks > 1:
        lax.fori_loop(0, chunks, rows, 0)
    else:
        for half in range(2):
            part(2 * half, 2, slice(None))


def terms_kernel(group, sector, shift, weights, own, by_chip, by_core, left2, right2, z, far, vec2):
    odd = lax.rem(sector[0], 2)
    for p in range(LOCAL):
        vec2[1, p] = jnp.concatenate(halves(own[p]), axis=1)
        vec2[2 - 2 * odd, p] = jnp.concatenate(halves(by_core[p]), axis=1)
        vec2[2 * odd, p] = jnp.concatenate(halves(by_chip[p]), axis=1)
    for k in range(TERMS):
        source = shift[k] + 1
        lhs = left2[k]
        for q in range(LOCAL):
            r = right2[k, q]
            x = jnp.dot(vec2[source, q], jnp.concatenate([r, r], axis=0), preferred_element_type=f32)
            xh, xl = halves(x[:, :B] + x[:, B:])
            both = jnp.concatenate([xh, xl], axis=1)
            y = jnp.dot(lhs, jnp.concatenate([both, both], axis=0), preferred_element_type=f32)
            z[k * LOCAL + q] = y[:, :B] + y[:, B:]
    mix(group, weights, z, group[0] ^ 2, far, 1)


def direct_kernel(group, sector, weights, z, direct):
    mix(group, weights, z, group[0] ^ (1 + 2 * lax.rem(sector[0], 2)), direct, 2)


def relayed_kernel(group, sector, weights, z, after, relayed):
    mix(group, weights, z, group[0] ^ (3 - 2 * lax.rem(sector[0], 2)), relayed, 4)


def relay_kernel(relayed, far, out):
    for p in range(LOCAL):
        out[p] = relayed[p] + far[p]


def own_kernel(group, weights, z, own):
    mix(group, weights, z, group[0], own, 4)


def lane(row, j):
    at = lax.broadcasted_iota(jnp.int32, row.shape, 1) == j
    return jnp.sum(jnp.where(at, row, 0.0), axis=1, keepdims=True)


def put_lanes(values, more=()):
    at = lax.broadcasted_iota(jnp.int32, (1, B), 1)
    row = jnp.zeros((1, B), f32)
    for j, v in [*enumerate(values), *enumerate(more, THETA)]:
        row = jnp.where(at == j, v, row)
    return row


def lowest_root(lead, middle, const):
    root = jnp.sqrt(middle * middle - 4.0 * lead * const)
    return jnp.where(middle > 0, (-middle - root) / (2.0 * lead), 2.0 * const / (root - middle))


def ritz(sums, rayleigh, length):
    s_ic, c_i, curvature, correlation, spread = sums
    cross = 0.5 * (s_ic + c_i)
    lead = length * spread - correlation * correlation
    middle = -(length * curvature + spread * rayleigh - 2.0 * correlation * cross)
    const = rayleigh * curvature - cross * cross
    lowest = lowest_root(lead, middle, const)
    keep = curvature - lowest * spread
    add = lowest * correlation - cross
    norm = keep * keep * length + 2.0 * keep * add * correlation + add * add * spread
    factor = 1.0 / jnp.sqrt(norm)
    keep, add = keep * factor, add * factor
    rayleigh = keep * keep * rayleigh + 2.0 * keep * add * cross + add * add * curvature
    length = keep * keep * length + 2.0 * keep * add * correlation + add * add * spread
    return lowest, keep, add, rayleigh, length


def totals(stats, count, n):
    row = jnp.sum(stats[...], axis=0, keepdims=True) * (1.0 / count)
    return [lane(row, j) for j in range(n)]


def correct(state, image, diag, theta):
    return (image - theta * state) / jnp.maximum(jnp.abs(diag - theta), 1.0)


def first_coefficients_kernel(count, stats, carry):
    rayleigh, length = totals(stats, count, 2)
    row = put_lanes([rayleigh, length], (rayleigh / length,))
    carry[...] = jnp.broadcast_to(row, (8, B))


def coefficients_kernel(count, step, stats, carry_in, carry):
    sums = totals(stats, count, 5)
    old = carry_in[0:1, :]
    lowest, keep, add, rayleigh, length = ritz(sums, lane(old, 0), lane(old, 1))
    energies = [lane(old, 2 + j) for j in range(step)] + [lowest]
    row = put_lanes([rayleigh, length] + energies, (rayleigh / length, keep, add))
    carry[...] = jnp.broadcast_to(row, (8, B))


def start_kernel(carry, s0, s1, s2, pack0, pack1, pack2, diag0, right_diag,
                 i0, i1, i2, diag1, diag2, c0, c1, c2):
    theta = lane(carry[0:1, :], THETA)
    for pack, diag in ((pack1, diag1), (pack2, diag2)):
        for p in range(LOCAL):
            diag[p] = outer(pack[LOCAL * B:PACK - 8, :], right_diag[p])
    for s, pack, i, diag, c in ((s0, pack0, i0, diag0, c0), (s1, pack1, i1, diag1, c1), (s2, pack2, i2, diag2, c2)):
        for p in range(LOCAL):
            block = pack[p * B:(p + 1) * B, :]
            i[p] = block
            c[p] = correct(s[p], block, diag[p], theta)


def next_kernel(keeps, carry, *refs):
    theta, keep, add = [lane(carry[0:1, :], THETA + j) for j in range(3)]
    for n in range(3):
        state, image, corr, diag, more = refs[n:15:3]
        for p in range(LOCAL):
            s = keep * state[p] + add * corr[p]
            i = keep * image[p] + add * more[p * B:(p + 1) * B, :]
            refs[15 + n][p] = correct(s, i, diag[p], theta)
            if n < keeps:
                refs[18 + n][p] = s
                refs[18 + keeps + n][p] = i

def last_kernel(count, stats, carry_in, state, corr, state_out, energies):
    sums = totals(stats, count, 5)
    old = carry_in[0:1, :]
    lowest, keep, add, _, _ = ritz(sums, lane(old, 0), lane(old, 1))
    for p in range(LOCAL):
        state_out[p] = keep * state[p] + add * corr[p]
    for j, v in enumerate([lane(old, 2 + j) for j in range(ITERS - 1)] + [lowest]):
        energies[j] = v[0, 0]


def sum_all(block):
    return jnp.sum(jnp.sum(block, axis=0, keepdims=True), axis=1, keepdims=True)


def first_stats_kernel(own, direct, relayed, state, left_diag, pack):
    a, b = jnp.zeros((B, B), f32), jnp.zeros((B, B), f32)
    for p in range(LOCAL):
        i = own[p] + (direct[p] + relayed[p])
        s = state[p]
        pack[p * B:(p + 1) * B, :] = i
        a = a + s * i
        b = b + s * s
    pack[LOCAL * B:PACK - 8, :] = left_diag[...]
    pack[PACK - 8:PACK, :] = jnp.broadcast_to(put_lanes([sum_all(a), sum_all(b)]), (8, B))


def stats_kernel(own, direct, relayed, state, corr, image, out):
    last = out.shape[0] <= LOCAL * B
    acc = [jnp.zeros((B, B), f32) for _ in range(5)]
    for p in range(LOCAL):
        ic = own[p] + (direct[p] + relayed[p])
        s, c, i = state[p], corr[p], image[p]
        if not last:
            out[p * B:(p + 1) * B, :] = ic
        for j, v in enumerate((s * ic, c * i, c * ic, s * c, c * c)):
            acc[j] = acc[j] + v
    row = put_lanes([sum_all(a) for a in acc])
    if last:
        out[...] = jnp.broadcast_to(row, out.shape)
    else:
        out[LOCAL * B:, :] = jnp.broadcast_to(row, (8, B))


def cores_kernel(mine, theirs, stats):
    at = mine.shape[0] - 8
    row = mine[at:at + 1, :] + theirs[at:at + 1, :]
    stats[...] = jnp.broadcast_to(row, stats.shape)


def arr(*shape, dtype=f32):
    return jax.ShapeDtypeStruct(shape, dtype)


BLOCK = arr(LOCAL, B, B)
TERM_BLOCKS = arr(TERMS * LOCAL, B, B)


def call(kernel, name, in_specs, outs, scratch=(), out_specs=None, flops=0):
    moved = sum(o.size * o.dtype.itemsize for o in outs)
    return pl.pallas_call(
        kernel,
        out_shape=outs,
        in_specs=in_specs,
        out_specs=out_specs or [VM] * len(outs),
        scratch_shapes=list(scratch),
        compiler_params=PARAMS,
        cost_estimate=pl.CostEstimate(flops=flops, bytes_accessed=2 * moved, transcendentals=0),
        name=name,
    )


def swap(x, even, odd):
    n = lax.axis_size("sec")
    perm = [(s * GROUPS + g, s * GROUPS + (g ^ (odd if s % 2 else even))) for s in range(n) for g in range(GROUPS)]
    return lax.ppermute(x, ("sec", "pair"), perm)


def from_chip(x):
    n = lax.axis_size("sec")
    return lax.ppermute(x, "sec", [(i, i + 1 if i % 2 else i - 1) for i in range(1, n - 1)])


def from_core(x):
    return lax.ppermute(x, "sec", [(i, i ^ 1) for i in range(lax.axis_size("sec"))])


def exchange(stats):
    return lax.all_to_all(stats.reshape(-1, 1, B), ("sec", "pair"), 0, 0).reshape(stats.shape)


def exchange_cores(mine, theirs):
    n = lax.axis_size("sec")
    groups = [[s * GROUPS + g for s in range(core, n, 2) for g in range(GROUPS)] for core in range(2)]
    (stats,) = call(cores_kernel, "cores", [VM] * 2, [arr(n // 2 * GROUPS, B)])(mine, theirs)
    got = lax.all_to_all(stats.reshape(-1, 1, B), ("sec", "pair"), 0, 0, axis_index_groups=groups)
    return got.reshape(stats.shape)


def on_device(psi_start, left_env, right_env, mpo_coef, mpo_pattern, sector_shift, block_rows):
    devices = lax.axis_size("sec") * lax.axis_size("pair")
    count = float(psi_start.size * devices)
    psi = psi_start.reshape(LOCAL, B, B)
    left = left_env.reshape(TERMS, B, B)
    group = lax.axis_index("pair").astype(jnp.int32).reshape(1)
    sector = lax.axis_index("sec").astype(jnp.int32).reshape(1)
    weights = (mpo_coef * mpo_pattern.astype(f32)).reshape(-1)
    carry_shape = arr(8, B)

    def shares(vectors, left2, right2):
        z, far = call(
            terms_kernel, "terms", [SM] * 4 + [VM] * 5, [TERM_BLOCKS, BLOCK],
            [pltpu.VMEM((3, LOCAL, B, 2 * B), bf16)],
        )(group, sector, sector_shift, weights, *vectors, left2, right2)
        far = swap(far, 1, 3)
        (direct,) = call(direct_kernel, "direct", [SM] * 3 + [VM], [BLOCK])(group, sector, weights, z)
        (relayed,) = call(relayed_kernel, "relayed", [SM] * 3 + [VM, ANY], [BLOCK])(group, sector, weights, z, direct)
        direct = swap(direct, 1, 3)
        (relayed,) = call(relay_kernel, "relay", [VM] * 2, [BLOCK])(relayed, far)
        (own,) = call(own_kernel, "own", [SM, SM, VM], [BLOCK])(group, weights, z)
        return own, direct, swap(relayed, 3, 1)

    (state,) = call(mask_kernel, "mask", [SM, VM], [BLOCK])(block_rows, psi)
    states = (state, from_chip(state), from_core(state))
    left2, right2, diag, left_diag, right_diag = call(
        split_kernel, "split", [SM] * 4 + [VM] * 2,
        [arr(TERMS, B, 2 * B, dtype=bf16), arr(TERMS, LOCAL, B, 2 * B, dtype=bf16), BLOCK, arr(8, B), arr(LOCAL, 8, B)],
    )(group, sector_shift, block_rows, weights, left, right_env)

    parts = shares(states, left2, right2)
    (pack,) = call(first_stats_kernel, "first_stats", [VM] * 5, [arr(PACK, B)])(*parts, state, left_diag)
    core = from_core(pack)
    got = exchange_cores(pack, core)
    packs = (pack, from_chip(pack), core)
    (carry,) = call(functools.partial(first_coefficients_kernel, count), "coefficients", [VM], [carry_shape])(got)
    out = call(start_kernel, "start", [VM] * 9, [BLOCK] * 8)(carry, *states, *packs, diag, right_diag)
    images, diags, corrs = out[:3], (diag, *out[3:5]), out[5:8]

    for step in range(ITERS):
        parts = shares(corrs, left2, right2)
        rows = LOCAL * B + 8 if step < ITERS - 1 else devices
        (out,) = call(stats_kernel, "stats", [VM] * 6, [arr(rows, B)])(*parts, states[0], corrs[0], images[0])
        if step == ITERS - 1:
            got = exchange(out)
        else:
            core = from_core(out)
            got = exchange_cores(out, core)
            more = (out, from_chip(out), core)
            keeps = 3 if step < ITERS - 2 else 1
            (carry,) = call(
                functools.partial(coefficients_kernel, count, step), "coefficients", [VM] * 2, [carry_shape]
            )(got, carry)
            out = call(functools.partial(next_kernel, keeps), "next", [VM] * 16, [BLOCK] * (3 + 2 * keeps))(
                carry, *states, *images, *corrs, *diags, *more)
            corrs, states, images = out[:3], out[3:3 + keeps], out[3 + keeps:]

    state, energies = call(
        lambda *refs: last_kernel(count, *refs), "last", [VM] * 4, [BLOCK, arr(ITERS)], out_specs=[VM, SM]
    )(got, carry, states[0], corrs[0])
    return state.reshape(psi_start.shape), energies


def solution(mesh):
    in_specs = (
        P("sec", "pair", None, None),
        P(None, "sec", None, None),
        P(None, "pair", None, None),
        P(),
        P(),
        P(),
        P("sec"),
    )
    out_specs = (P("sec", "pair", None, None), P())
    return jax.shard_map(
        on_device, mesh=mesh, in_specs=in_specs, out_specs=out_specs, check_vma=False
    )
```

```python
import functools

import jax
import jax.numpy as jnp
from jax import lax
from jax.experimental import pallas as pl
from jax.experimental.pallas import tpu as pltpu
from jax.sharding import PartitionSpec as P

ITERS = 4
TERMS = 6
LOCAL = 4
GROUPS = 4
B = 128
PACK = LOCAL * B + 16
THETA = 16
SHIFTS = TERMS * 16 * 16

f32 = jnp.float32
bf16 = jnp.bfloat16
VM = pl.BlockSpec(memory_space=pltpu.VMEM)
SM = pl.BlockSpec(memory_space=pltpu.SMEM)
ANY = pl.BlockSpec(memory_space=pl.ANY)
PARAMS = pltpu.CompilerParams(vmem_limit_bytes=24 * 1024 * 1024)


def halves(x):
    high = x.astype(bf16)
    return high, (x - high.astype(f32)).astype(bf16)


def eye_mask():
    return lax.broadcasted_iota(jnp.int32, (B, B), 0) == lax.broadcasted_iota(jnp.int32, (B, B), 1)


def row_mask(rows):
    return (lax.broadcasted_iota(jnp.int32, (B, B), 0) < rows[0]).astype(f32)


def mask_kernel(rows, psi, state):
    keep = row_mask(rows)
    for p in range(LOCAL):
        state[p] = psi[p] * keep


def outer(left_lines, right_lines):
    return lax.dot_general(
        left_lines, right_lines, (((0,), (0,)), ((), ())),
        precision=lax.Precision.HIGHEST, preferred_element_type=f32)


def split_kernel(group, rows, weights, left, right, left2, right2, diag, left_diag, right_diag):
    keep = row_mask(rows)
    eye = eye_mask()
    pad = jnp.zeros((8 - TERMS, B), f32)
    lines = []
    for k in range(TERMS):
        block = left[k] * keep
        left2[k] = jnp.concatenate(halves(block), axis=1)
        chosen = jnp.where(weights[SHIFTS + k] == 0.0, 1.0, 0.0).astype(f32)
        lines.append(jnp.sum(jnp.where(eye, block, 0.0), axis=0, keepdims=True) * chosen)
    left_diag[...] = jnp.concatenate(lines + [pad], axis=0)
    lines = [[] for _ in range(LOCAL)]
    for k in range(TERMS):
        for q in range(LOCAL):
            block = right[k, q]
            right2[k, q] = jnp.concatenate(halves(jnp.transpose(block)), axis=1)
            p = group[0] * LOCAL + q
            scale = weights[k * 256 + p * 16 + p]
            lines[q].append(jnp.sum(jnp.where(eye, block, 0.0), axis=0, keepdims=True) * scale)
    for q in range(LOCAL):
        right_diag[q] = jnp.concatenate(lines[q] + [pad], axis=0)
        diag[q] = outer(left_diag[...], right_diag[q])


def mix(group, weights, z, target, out, chunks):
    height = B // chunks

    def part(start, width, at):
        first = target * LOCAL + start
        acc = [None] * width
        for k in range(TERMS):
            for q in range(LOCAL):
                block = z[k * LOCAL + q, at, :]
                for j in range(width):
                    term = weights[k * 256 + (first + j) * 16 + group[0] * LOCAL + q] * block
                    acc[j] = term if acc[j] is None else acc[j] + term
        for j in range(width):
            out[start + j, at, :] = acc[j]

    def rows(r, carry):
        part(0, LOCAL, pl.ds(pl.multiple_of(r * height, height), height))
        return carry

    if chunks > 1:
        lax.fori_loop(0, chunks, rows, 0)
    else:
        for half in range(2):
            part(2 * half, 2, slice(None))


def terms_kernel(group, sector, weights, own, by_chip, by_core, left2, right2, z, far, vec2):
    odd = lax.rem(sector[0], 2)
    for p in range(LOCAL):
        vec2[1, p] = jnp.concatenate(halves(own[p]), axis=1)
        vec2[2 - 2 * odd, p] = jnp.concatenate(halves(by_core[p]), axis=1)
        vec2[2 * odd, p] = jnp.concatenate(halves(by_chip[p]), axis=1)
    for k in range(TERMS):
        source = weights[SHIFTS + k].astype(jnp.int32) + 1
        lhs = left2[k]
        for q in range(LOCAL):
            r = right2[k, q]
            x = jnp.dot(vec2[source, q], jnp.concatenate([r, r], axis=0), preferred_element_type=f32)
            xh, xl = halves(x[:, :B] + x[:, B:])
            both = jnp.concatenate([xh, xl], axis=1)
            y = jnp.dot(lhs, jnp.concatenate([both, both], axis=0), preferred_element_type=f32)
            z[k * LOCAL + q] = y[:, :B] + y[:, B:]
    mix(group, weights, z, group[0] ^ 2, far, 1)


def direct_kernel(group, sector, weights, z, direct):
    mix(group, weights, z, group[0] ^ (1 + 2 * lax.rem(sector[0], 2)), direct, 2)


def relayed_kernel(group, sector, weights, z, after, relayed):
    mix(group, weights, z, group[0] ^ (3 - 2 * lax.rem(sector[0], 2)), relayed, 4)


def relay_kernel(relayed, far, out):
    for p in range(LOCAL):
        out[p] = relayed[p] + far[p]


def own_kernel(group, weights, z, own):
    mix(group, weights, z, group[0], own, 4)


def lane(row, j):
    at = lax.broadcasted_iota(jnp.int32, row.shape, 1) == j
    return jnp.sum(jnp.where(at, row, 0.0), axis=1, keepdims=True)


def put_lanes(values, more=()):
    at = lax.broadcasted_iota(jnp.int32, (1, B), 1)
    row = jnp.zeros((1, B), f32)
    for j, v in [*enumerate(values), *enumerate(more, THETA)]:
        row = jnp.where(at == j, v, row)
    return row


def lowest_root(lead, middle, const):
    root = jnp.sqrt(middle * middle - 4.0 * lead * const)
    return jnp.where(middle > 0, (-middle - root) / (2.0 * lead), 2.0 * const / (root - middle))


def ritz(sums, rayleigh, length):
    s_ic, c_i, curvature, correlation, spread = sums
    cross = 0.5 * (s_ic + c_i)
    lead = length * spread - correlation * correlation
    middle = -(length * curvature + spread * rayleigh - 2.0 * correlation * cross)
    const = rayleigh * curvature - cross * cross
    lowest = lowest_root(lead, middle, const)
    keep = curvature - lowest * spread
    add = lowest * correlation - cross
    norm = keep * keep * length + 2.0 * keep * add * correlation + add * add * spread
    factor = 1.0 / jnp.sqrt(norm)
    keep, add = keep * factor, add * factor
    rayleigh = keep * keep * rayleigh + 2.0 * keep * add * cross + add * add * curvature
    length = keep * keep * length + 2.0 * keep * add * correlation + add * add * spread
    return lowest, keep, add, rayleigh, length


def totals(stats, count, n):
    row = jnp.sum(stats[...], axis=0, keepdims=True) * (1.0 / count)
    return [lane(row, j) for j in range(n)]


def correct(state, image, diag, theta):
    return (image - theta * state) / jnp.maximum(jnp.abs(diag - theta), 1.0)


def first_coefficients_kernel(count, stats, carry):
    rayleigh, length = totals(stats, count, 2)
    row = put_lanes([rayleigh, length], (rayleigh / length,))
    carry[...] = jnp.broadcast_to(row, (8, B))


def coefficients_kernel(count, step, stats, carry_in, carry):
    sums = totals(stats, count, 5)
    old = carry_in[0:1, :]
    lowest, keep, add, rayleigh, length = ritz(sums, lane(old, 0), lane(old, 1))
    energies = [lane(old, 2 + j) for j in range(step)] + [lowest]
    row = put_lanes([rayleigh, length] + energies, (rayleigh / length, keep, add))
    carry[...] = jnp.broadcast_to(row, (8, B))


def start_kernel(carry, s0, s1, s2, pack0, pack1, pack2, diag0, right_diag,
                 i0, i1, i2, diag1, diag2, c0, c1, c2):
    theta = lane(carry[0:1, :], THETA)
    for pack, diag in ((pack1, diag1), (pack2, diag2)):
        for p in range(LOCAL):
            diag[p] = outer(pack[LOCAL * B:PACK - 8, :], right_diag[p])
    for s, pack, i, diag, c in ((s0, pack0, i0, diag0, c0), (s1, pack1, i1, diag1, c1), (s2, pack2, i2, diag2, c2)):
        for p in range(LOCAL):
            block = pack[p * B:(p + 1) * B, :]
            i[p] = block
            c[p] = correct(s[p], block, diag[p], theta)


def next_kernel(keeps, carry, *refs):
    theta, keep, add = [lane(carry[0:1, :], THETA + j) for j in range(3)]
    for n in range(3):
        state, image, corr, diag, more = refs[n:15:3]
        for p in range(LOCAL):
            s = keep * state[p] + add * corr[p]
            i = keep * image[p] + add * more[p * B:(p + 1) * B, :]
            refs[15 + n][p] = correct(s, i, diag[p], theta)
            if n < keeps:
                refs[18 + n][p] = s
                refs[18 + keeps + n][p] = i

def last_kernel(count, stats, carry_in, state, corr, state_out, energies):
    sums = totals(stats, count, 5)
    old = carry_in[0:1, :]
    lowest, keep, add, _, _ = ritz(sums, lane(old, 0), lane(old, 1))
    for p in range(LOCAL):
        state_out[p] = keep * state[p] + add * corr[p]
    for j, v in enumerate([lane(old, 2 + j) for j in range(ITERS - 1)] + [lowest]):
        energies[j] = v[0, 0]


def sum_all(block):
    return jnp.sum(jnp.sum(block, axis=0, keepdims=True), axis=1, keepdims=True)


def first_stats_kernel(own, direct, relayed, state, left_diag, pack):
    a, b = jnp.zeros((B, B), f32), jnp.zeros((B, B), f32)
    for p in range(LOCAL):
        i = own[p] + (direct[p] + relayed[p])
        s = state[p]
        pack[p * B:(p + 1) * B, :] = i
        a = a + s * i
        b = b + s * s
    pack[LOCAL * B:PACK - 8, :] = left_diag[...]
    pack[PACK - 8:PACK, :] = jnp.broadcast_to(put_lanes([sum_all(a), sum_all(b)]), (8, B))


def stats_kernel(own, direct, relayed, state, corr, image, out):
    last = out.shape[0] <= LOCAL * B
    acc = [jnp.zeros((B, B), f32) for _ in range(5)]
    for p in range(LOCAL):
        ic = own[p] + (direct[p] + relayed[p])
        s, c, i = state[p], corr[p], image[p]
        if not last:
            out[p * B:(p + 1) * B, :] = ic
        for j, v in enumerate((s * ic, c * i, c * ic, s * c, c * c)):
            acc[j] = acc[j] + v
    row = put_lanes([sum_all(a) for a in acc])
    if last:
        out[...] = jnp.broadcast_to(row, out.shape)
    else:
        out[LOCAL * B:, :] = jnp.broadcast_to(row, (8, B))


def cores_kernel(mine, theirs, stats):
    at = mine.shape[0] - 8
    row = mine[at:at + 1, :] + theirs[at:at + 1, :]
    stats[...] = jnp.broadcast_to(row, stats.shape)


def arr(*shape, dtype=f32):
    return jax.ShapeDtypeStruct(shape, dtype)


BLOCK = arr(LOCAL, B, B)
TERM_BLOCKS = arr(TERMS * LOCAL, B, B)


def call(kernel, name, in_specs, outs, scratch=(), out_specs=None, flops=0):
    moved = sum(o.size * o.dtype.itemsize for o in outs)
    return pl.pallas_call(
        kernel,
        out_shape=outs,
        in_specs=in_specs,
        out_specs=out_specs or [VM] * len(outs),
        scratch_shapes=list(scratch),
        compiler_params=PARAMS,
        cost_estimate=pl.CostEstimate(flops=flops, bytes_accessed=2 * moved, transcendentals=0),
        name=name,
    )


def swap(x, even, odd):
    n = lax.axis_size("sec")
    perm = [(s * GROUPS + g, s * GROUPS + (g ^ (odd if s % 2 else even))) for s in range(n) for g in range(GROUPS)]
    return lax.ppermute(x, ("sec", "pair"), perm)


def from_chip(x):
    n = lax.axis_size("sec")
    return lax.ppermute(x, "sec", [(i, i + 1 if i % 2 else i - 1) for i in range(1, n - 1)])


def from_core(x):
    return lax.ppermute(x, "sec", [(i, i ^ 1) for i in range(lax.axis_size("sec"))])


def exchange(stats):
    return lax.all_to_all(stats.reshape(-1, 1, B), ("sec", "pair"), 0, 0).reshape(stats.shape)


def exchange_cores(mine, theirs):
    n = lax.axis_size("sec")
    groups = [[s * GROUPS + g for s in range(core, n, 2) for g in range(GROUPS)] for core in range(2)]
    (stats,) = call(cores_kernel, "cores", [VM] * 2, [arr(n // 2 * GROUPS, B)])(mine, theirs)
    got = lax.all_to_all(stats.reshape(-1, 1, B), ("sec", "pair"), 0, 0, axis_index_groups=groups)
    return got.reshape(stats.shape)


def on_device(psi_start, left_env, right_env, mpo_coef, mpo_pattern, sector_shift, block_rows):
    devices = lax.axis_size("sec") * lax.axis_size("pair")
    count = float(psi_start.size * devices)
    psi = psi_start.reshape(LOCAL, B, B)
    left = left_env.reshape(TERMS, B, B)
    group = lax.axis_index("pair").astype(jnp.int32).reshape(1)
    sector = lax.axis_index("sec").astype(jnp.int32).reshape(1)
    weights = (mpo_coef * mpo_pattern.astype(f32)).reshape(-1)
    weights = jnp.concatenate([weights, sector_shift.astype(f32)])
    carry_shape = arr(8, B)

    def shares(vectors, left2, right2):
        z, far = call(
            terms_kernel, "terms", [SM] * 3 + [VM] * 5, [TERM_BLOCKS, BLOCK],
            [pltpu.VMEM((3, LOCAL, B, 2 * B), bf16)],
        )(group, sector, weights, *vectors, left2, right2)
        far = swap(far, 1, 3)
        (direct,) = call(direct_kernel, "direct", [SM] * 3 + [VM], [BLOCK])(group, sector, weights, z)
        (relayed,) = call(relayed_kernel, "relayed", [SM] * 3 + [VM, ANY], [BLOCK])(group, sector, weights, z, direct)
        direct = swap(direct, 1, 3)
        (relayed,) = call(relay_kernel, "relay", [VM] * 2, [BLOCK])(relayed, far)
        (own,) = call(own_kernel, "own", [SM, SM, VM], [BLOCK])(group, weights, z)
        return own, direct, swap(relayed, 3, 1)

    (state,) = call(mask_kernel, "mask", [SM, VM], [BLOCK])(block_rows, psi)
    states = (state, from_chip(state), from_core(state))
    left2, right2, diag, left_diag, right_diag = call(
        split_kernel, "split", [SM] * 3 + [VM] * 2,
        [arr(TERMS, B, 2 * B, dtype=bf16), arr(TERMS, LOCAL, B, 2 * B, dtype=bf16), BLOCK, arr(8, B), arr(LOCAL, 8, B)],
    )(group, block_rows, weights, left, right_env)

    parts = shares(states, left2, right2)
    (pack,) = call(first_stats_kernel, "first_stats", [VM] * 5, [arr(PACK, B)])(*parts, state, left_diag)
    core = from_core(pack)
    got = exchange_cores(pack, core)
    packs = (pack, from_chip(pack), core)
    (carry,) = call(functools.partial(first_coefficients_kernel, count), "coefficients", [VM], [carry_shape])(got)
    out = call(start_kernel, "start", [VM] * 9, [BLOCK] * 8)(carry, *states, *packs, diag, right_diag)
    images, diags, corrs = out[:3], (diag, *out[3:5]), out[5:8]

    for step in range(ITERS):
        parts = shares(corrs, left2, right2)
        rows = LOCAL * B + 8 if step < ITERS - 1 else devices
        (out,) = call(stats_kernel, "stats", [VM] * 6, [arr(rows, B)])(*parts, states[0], corrs[0], images[0])
        if step == ITERS - 1:
            got = exchange(out)
        else:
            core = from_core(out)
            got = exchange_cores(out, core)
            more = (out, from_chip(out), core)
            keeps = 3 if step < ITERS - 2 else 1
            (carry,) = call(
                functools.partial(coefficients_kernel, count, step), "coefficients", [VM] * 2, [carry_shape]
            )(got, carry)
            out = call(functools.partial(next_kernel, keeps), "next", [VM] * 16, [BLOCK] * (3 + 2 * keeps))(
                carry, *states, *images, *corrs, *diags, *more)
            corrs, states, images = out[:3], out[3:3 + keeps], out[3 + keeps:]

    state, energies = call(
        lambda *refs: last_kernel(count, *refs), "last", [VM] * 4, [BLOCK, arr(ITERS)], out_specs=[VM, SM]
    )(got, carry, states[0], corrs[0])
    return state.reshape(psi_start.shape), energies


def solution(mesh):
    in_specs = (
        P("sec", "pair", None, None),
        P(None, "sec", None, None),
        P(None, "pair", None, None),
        P(),
        P(),
        P(),
        P("sec"),
    )
    out_specs = (P("sec", "pair", None, None), P())
    return jax.shard_map(
        on_device, mesh=mesh, in_specs=in_specs, out_specs=out_specs, check_vma=False
    )
```

```python
import functools

import jax
import jax.numpy as jnp
from jax import lax
from jax.experimental import pallas as pl
from jax.experimental.pallas import tpu as pltpu
from jax.sharding import PartitionSpec as P

ITERS = 4
TERMS = 6
LOCAL = 4
GROUPS = 4
B = 128
PACK = LOCAL * B + 16
THETA = 16
SHIFTS = TERMS * 16 * 16

f32 = jnp.float32
bf16 = jnp.bfloat16
VM = pl.BlockSpec(memory_space=pltpu.VMEM)
SM = pl.BlockSpec(memory_space=pltpu.SMEM)
ANY = pl.BlockSpec(memory_space=pl.ANY)
PARAMS = pltpu.CompilerParams(vmem_limit_bytes=24 * 1024 * 1024)


def halves(x):
    high = x.astype(bf16)
    return high, (x - high.astype(f32)).astype(bf16)


def eye_mask():
    return lax.broadcasted_iota(jnp.int32, (B, B), 0) == lax.broadcasted_iota(jnp.int32, (B, B), 1)


def row_mask(rows):
    return (lax.broadcasted_iota(jnp.int32, (B, B), 0) < rows[0]).astype(f32)


def mask_kernel(rows, psi, state):
    keep = row_mask(rows)
    for p in range(LOCAL):
        state[p] = psi[p] * keep


def outer(left_lines, right_lines):
    return lax.dot_general(
        left_lines, right_lines, (((0,), (0,)), ((), ())),
        precision=lax.Precision.HIGHEST, preferred_element_type=f32)


def split_kernel(group, rows, weights, left, right, left2, right2, diag, left_diag, right_diag):
    keep = row_mask(rows)
    eye = eye_mask()
    pad = jnp.zeros((8 - TERMS, B), f32)
    lines = []
    for k in range(TERMS):
        block = left[k] * keep
        left2[k] = jnp.concatenate(halves(block), axis=1)
        chosen = jnp.where(weights[SHIFTS + k] == 0.0, 1.0, 0.0).astype(f32)
        lines.append(jnp.sum(jnp.where(eye, block, 0.0), axis=0, keepdims=True) * chosen)
    left_diag[...] = jnp.concatenate(lines + [pad], axis=0)
    lines = [[] for _ in range(LOCAL)]
    for k in range(TERMS):
        for q in range(LOCAL):
            block = right[k, q]
            right2[k, q] = jnp.concatenate(halves(jnp.transpose(block)), axis=1)
            p = group[0] * LOCAL + q
            scale = weights[k * 256 + p * 16 + p]
            lines[q].append(jnp.sum(jnp.where(eye, block, 0.0), axis=0, keepdims=True) * scale)
    for q in range(LOCAL):
        right_diag[q] = jnp.concatenate(lines[q] + [pad], axis=0)
        diag[q] = outer(left_diag[...], right_diag[q])


def mix(group, weights, z, target, out, chunks):
    height = B // chunks

    def part(start, width, at):
        first = target * LOCAL + start
        acc = [None] * width
        for k in range(TERMS):
            for q in range(LOCAL):
                block = z[k * LOCAL + q, at, :]
                for j in range(width):
                    term = weights[k * 256 + (first + j) * 16 + group[0] * LOCAL + q] * block
                    acc[j] = term if acc[j] is None else acc[j] + term
        for j in range(width):
            out[start + j, at, :] = acc[j]

    def rows(r, carry):
        part(0, LOCAL, pl.ds(pl.multiple_of(r * height, height), height))
        return carry

    if chunks > 1:
        lax.fori_loop(0, chunks, rows, 0)
    else:
        for half in range(2):
            part(2 * half, 2, slice(None))


def terms_kernel(group, sector, weights, own, by_chip, by_core, left2, right2, z, far, vec2):
    odd = lax.rem(sector[0], 2)
    for p in range(LOCAL):
        vec2[1, p] = jnp.concatenate(halves(own[p]), axis=1)
        vec2[2 - 2 * odd, p] = jnp.concatenate(halves(by_core[p]), axis=1)
        vec2[2 * odd, p] = jnp.concatenate(halves(by_chip[p]), axis=1)
    for k in range(TERMS):
        source = weights[SHIFTS + k].astype(jnp.int32) + 1
        lhs = left2[k]
        for q in range(LOCAL):
            r = right2[k, q]
            x = jnp.dot(vec2[source, q], jnp.concatenate([r, r], axis=0), preferred_element_type=f32)
            xh, xl = halves(x[:, :B] + x[:, B:])
            both = jnp.concatenate([xh, xl], axis=1)
            y = jnp.dot(lhs, jnp.concatenate([both, both], axis=0), preferred_element_type=f32)
            z[k * LOCAL + q] = y[:, :B] + y[:, B:]
    mix(group, weights, z, group[0] ^ 2, far, 1)


def direct_kernel(group, sector, weights, z, direct):
    mix(group, weights, z, group[0] ^ (1 + 2 * lax.rem(sector[0], 2)), direct, 2)


def relayed_kernel(group, sector, weights, z, after, relayed):
    mix(group, weights, z, group[0] ^ (3 - 2 * lax.rem(sector[0], 2)), relayed, 4)


def relay_kernel(relayed, far, out):
    for p in range(LOCAL):
        out[p] = relayed[p] + far[p]


def own_kernel(group, weights, z, own):
    mix(group, weights, z, group[0], own, 4)


def lane(row, j):
    at = lax.broadcasted_iota(jnp.int32, row.shape, 1) == j
    return jnp.sum(jnp.where(at, row, 0.0), axis=1, keepdims=True)


def put_lanes(values, more=()):
    at = lax.broadcasted_iota(jnp.int32, (1, B), 1)
    row = jnp.zeros((1, B), f32)
    for j, v in [*enumerate(values), *enumerate(more, THETA)]:
        row = jnp.where(at == j, v, row)
    return row


def lowest_root(lead, middle, const):
    root = jnp.sqrt(middle * middle - 4.0 * lead * const)
    return jnp.where(middle > 0, (-middle - root) / (2.0 * lead), 2.0 * const / (root - middle))


def ritz(sums, rayleigh, length):
    s_ic, c_i, curvature, correlation, spread = sums
    cross = 0.5 * (s_ic + c_i)
    lead = length * spread - correlation * correlation
    middle = -(length * curvature + spread * rayleigh - 2.0 * correlation * cross)
    const = rayleigh * curvature - cross * cross
    lowest = lowest_root(lead, middle, const)
    keep = curvature - lowest * spread
    add = lowest * correlation - cross
    norm = keep * keep * length + 2.0 * keep * add * correlation + add * add * spread
    factor = 1.0 / jnp.sqrt(norm)
    keep, add = keep * factor, add * factor
    rayleigh = keep * keep * rayleigh + 2.0 * keep * add * cross + add * add * curvature
    length = keep * keep * length + 2.0 * keep * add * correlation + add * add * spread
    return lowest, keep, add, rayleigh, length


def totals(stats, count, n):
    row = jnp.sum(stats[...], axis=0, keepdims=True) * (1.0 / count)
    return [lane(row, j) for j in range(n)]


def correct(state, image, diag, theta):
    return (image - theta * state) / jnp.maximum(jnp.abs(diag - theta), 1.0)


def first_coefficients_kernel(count, stats, carry):
    rayleigh, length = totals(stats, count, 2)
    row = put_lanes([rayleigh, length], (rayleigh / length,))
    carry[...] = jnp.broadcast_to(row, (8, B))


def coefficients_kernel(count, step, stats, carry_in, carry):
    sums = totals(stats, count, 5)
    old = carry_in[0:1, :]
    lowest, keep, add, rayleigh, length = ritz(sums, lane(old, 0), lane(old, 1))
    energies = [lane(old, 2 + j) for j in range(step)] + [lowest]
    row = put_lanes([rayleigh, length] + energies, (rayleigh / length, keep, add))
    carry[...] = jnp.broadcast_to(row, (8, B))


def start_kernel(carry, s0, s1, s2, pack0, pack1, pack2, diag0, right_diag,
                 i0, i1, i2, diag1, diag2, c0, c1, c2):
    theta = lane(carry[0:1, :], THETA)
    for pack, diag in ((pack1, diag1), (pack2, diag2)):
        for p in range(LOCAL):
            diag[p] = outer(pack[LOCAL * B:PACK - 8, :], right_diag[p])
    for s, pack, i, diag, c in ((s0, pack0, i0, diag0, c0), (s1, pack1, i1, diag1, c1), (s2, pack2, i2, diag2, c2)):
        for p in range(LOCAL):
            block = pack[p * B:(p + 1) * B, :]
            i[p] = block
            c[p] = correct(s[p], block, diag[p], theta)


def next_kernel(keeps, carry, *refs):
    theta, keep, add = [lane(carry[0:1, :], THETA + j) for j in range(3)]
    for n in range(3):
        state, image, corr, diag, more = refs[n:15:3]
        for p in range(LOCAL):
            s = keep * state[p] + add * corr[p]
            i = keep * image[p] + add * more[p * B:(p + 1) * B, :]
            refs[15 + n][p] = correct(s, i, diag[p], theta)
            if n < keeps:
                refs[18 + n][p] = s
                refs[18 + keeps + n][p] = i

def last_kernel(count, stats, carry_in, state, corr, state_out, energies):
    sums = totals(stats, count, 5)
    old = carry_in[0:1, :]
    lowest, keep, add, _, _ = ritz(sums, lane(old, 0), lane(old, 1))
    for p in range(LOCAL):
        state_out[p] = keep * state[p] + add * corr[p]
    for j, v in enumerate([lane(old, 2 + j) for j in range(ITERS - 1)] + [lowest]):
        energies[j] = v[0, 0]


def sum_all(block):
    return jnp.sum(jnp.sum(block, axis=0, keepdims=True), axis=1, keepdims=True)


def first_stats_kernel(own, direct, relayed, state, left_diag, pack):
    a, b = jnp.zeros((B, B), f32), jnp.zeros((B, B), f32)
    for p in range(LOCAL):
        i = own[p] + (direct[p] + relayed[p])
        s = state[p]
        pack[p * B:(p + 1) * B, :] = i
        a = a + s * i
        b = b + s * s
    pack[LOCAL * B:PACK - 8, :] = left_diag[...]
    pack[PACK - 8:PACK, :] = jnp.broadcast_to(put_lanes([sum_all(a), sum_all(b)]), (8, B))


def stats_kernel(own, direct, relayed, state, corr, image, out):
    last = out.shape[0] <= LOCAL * B
    acc = [jnp.zeros((B, B), f32) for _ in range(5)]
    for p in range(LOCAL):
        ic = own[p] + (direct[p] + relayed[p])
        s, c, i = state[p], corr[p], image[p]
        if not last:
            out[p * B:(p + 1) * B, :] = ic
        for j, v in enumerate((s * ic, c * i, c * ic, s * c, c * c)):
            acc[j] = acc[j] + v
    row = put_lanes([sum_all(a) for a in acc])
    if last:
        out[...] = jnp.broadcast_to(row, out.shape)
    else:
        out[LOCAL * B:, :] = jnp.broadcast_to(row, (8, B))


def cores_kernel(mine, theirs, stats):
    at = mine.shape[0] - 8
    row = mine[at:at + 1, :] + theirs[at:at + 1, :]
    stats[...] = jnp.broadcast_to(row, stats.shape)


def arr(*shape, dtype=f32):
    return jax.ShapeDtypeStruct(shape, dtype)


BLOCK = arr(LOCAL, B, B)
TERM_BLOCKS = arr(TERMS * LOCAL, B, B)


def call(kernel, name, in_specs, outs, scratch=(), out_specs=None, flops=0):
    moved = sum(o.size * o.dtype.itemsize for o in outs)
    return pl.pallas_call(
        kernel,
        out_shape=outs,
        in_specs=in_specs,
        out_specs=out_specs or [VM] * len(outs),
        scratch_shapes=list(scratch),
        compiler_params=PARAMS,
        cost_estimate=pl.CostEstimate(flops=flops, bytes_accessed=2 * moved, transcendentals=0),
        name=name,
    )


def swap(x, even, odd):
    n = lax.axis_size("sec")
    perm = [(s * GROUPS + g, s * GROUPS + (g ^ (odd if s % 2 else even))) for s in range(n) for g in range(GROUPS)]
    return lax.ppermute(x, ("sec", "pair"), perm)


def from_chip(x):
    n = lax.axis_size("sec")
    return lax.ppermute(x, "sec", [(i, i + 1 if i % 2 else i - 1) for i in range(1, n - 1)])


def from_core(x):
    return lax.ppermute(x, "sec", [(i, i ^ 1) for i in range(lax.axis_size("sec"))])


def exchange_cores(mine, theirs):
    n = lax.axis_size("sec")
    groups = [[s * GROUPS + g for s in range(core, n, 2) for g in range(GROUPS)] for core in range(2)]
    (stats,) = call(cores_kernel, "cores", [VM] * 2, [arr(n // 2 * GROUPS, B)])(mine, theirs)
    got = lax.all_to_all(stats.reshape(-1, 1, B), ("sec", "pair"), 0, 0, axis_index_groups=groups)
    return got.reshape(stats.shape)


def on_device(psi_start, left_env, right_env, mpo_coef, mpo_pattern, sector_shift, block_rows):
    devices = lax.axis_size("sec") * lax.axis_size("pair")
    count = float(psi_start.size * devices)
    psi = psi_start.reshape(LOCAL, B, B)
    left = left_env.reshape(TERMS, B, B)
    group = lax.axis_index("pair").astype(jnp.int32).reshape(1)
    sector = lax.axis_index("sec").astype(jnp.int32).reshape(1)
    weights = (mpo_coef * mpo_pattern.astype(f32)).reshape(-1)
    weights = jnp.concatenate([weights, sector_shift.astype(f32)])
    carry_shape = arr(8, B)

    def shares(vectors, left2, right2):
        z, far = call(
            terms_kernel, "terms", [SM] * 3 + [VM] * 5, [TERM_BLOCKS, BLOCK],
            [pltpu.VMEM((3, LOCAL, B, 2 * B), bf16)],
        )(group, sector, weights, *vectors, left2, right2)
        far = swap(far, 1, 3)
        (direct,) = call(direct_kernel, "direct", [SM] * 3 + [VM], [BLOCK])(group, sector, weights, z)
        (relayed,) = call(relayed_kernel, "relayed", [SM] * 3 + [VM, ANY], [BLOCK])(group, sector, weights, z, direct)
        direct = swap(direct, 1, 3)
        (relayed,) = call(relay_kernel, "relay", [VM] * 2, [BLOCK])(relayed, far)
        (own,) = call(own_kernel, "own", [SM, SM, VM], [BLOCK])(group, weights, z)
        return own, direct, swap(relayed, 3, 1)

    (state,) = call(mask_kernel, "mask", [SM, VM], [BLOCK])(block_rows, psi)
    states = (state, from_chip(state), from_core(state))
    left2, right2, diag, left_diag, right_diag = call(
        split_kernel, "split", [SM] * 3 + [VM] * 2,
        [arr(TERMS, B, 2 * B, dtype=bf16), arr(TERMS, LOCAL, B, 2 * B, dtype=bf16), BLOCK, arr(8, B), arr(LOCAL, 8, B)],
    )(group, block_rows, weights, left, right_env)

    parts = shares(states, left2, right2)
    (pack,) = call(first_stats_kernel, "first_stats", [VM] * 5, [arr(PACK, B)])(*parts, state, left_diag)
    core = from_core(pack)
    got = exchange_cores(pack, core)
    packs = (pack, from_chip(pack), core)
    (carry,) = call(functools.partial(first_coefficients_kernel, count), "coefficients", [VM], [carry_shape])(got)
    out = call(start_kernel, "start", [VM] * 9, [BLOCK] * 8)(carry, *states, *packs, diag, right_diag)
    images, diags, corrs = out[:3], (diag, *out[3:5]), out[5:8]

    for step in range(ITERS):
        parts = shares(corrs, left2, right2)
        rows = LOCAL * B + 8 if step < ITERS - 1 else 8
        (out,) = call(stats_kernel, "stats", [VM] * 6, [arr(rows, B)])(*parts, states[0], corrs[0], images[0])
        core = from_core(out)
        got = exchange_cores(out, core)
        if step < ITERS - 1:
            more = (out, from_chip(out), core)
            keeps = 3 if step < ITERS - 2 else 1
            (carry,) = call(
                functools.partial(coefficients_kernel, count, step), "coefficients", [VM] * 2, [carry_shape]
            )(got, carry)
            out = call(functools.partial(next_kernel, keeps), "next", [VM] * 16, [BLOCK] * (3 + 2 * keeps))(
                carry, *states, *images, *corrs, *diags, *more)
            corrs, states, images = out[:3], out[3:3 + keeps], out[3 + keeps:]

    state, energies = call(
        lambda *refs: last_kernel(count, *refs), "last", [VM] * 4, [BLOCK, arr(ITERS)], out_specs=[VM, SM]
    )(got, carry, states[0], corrs[0])
    return state.reshape(psi_start.shape), energies


def solution(mesh):
    in_specs = (
        P("sec", "pair", None, None),
        P(None, "sec", None, None),
        P(None, "pair", None, None),
        P(),
        P(),
        P(),
        P("sec"),
    )
    out_specs = (P("sec", "pair", None, None), P())
    return jax.shard_map(
        on_device, mesh=mesh, in_specs=in_specs, out_specs=out_specs, check_vma=False
    )
```
